32 devices in a mesh: row: 4 (over x, core), col: 8 (over z, y).
Axes of the slice: x: 2, y: 2, z: 4, core: 2. Of those that a mesh axis runs over, the one named last changes fastest.
Arguments:
- start_block: float32 [65536, 128], P(('row', 'col')), may hold values from -6 to 6
- block_values: float32 [4, 16, 512, 512], P('row', 'col'), may hold values from -0.25 to 0.25
- block_rows: int32 [4, 16], P('row', 'col'), may hold values from 0 to 31, as said below
- block_cols: int32 [4, 16], P('row', 'col'), may hold values from 0 to 15
- block_count: int32 [4, 8], P('row', 'col'), may hold values from 1 to 2, as said below
- center: float32 [1], replicated, may hold values from 0.5 to 1
- radius: float32 [1], replicated, may hold values from 0.8 to 1.2
Outputs:
- basis_block: float32 [65536, 128], P(('row', 'col'))
- projected: float32 [128, 128], replicated
The draws below stay inside these ranges and needn't reach their ends.
Inputs may be any that keep to these rules, and one draw needn't show every extreme that they name: `block_rows`: block row within the tile; the used slots of one tile name distinct block positions. `block_count`: some tile holds exactly 2 used slots in every draw.
All inputs are finite; a program needn't handle non-finite values.
Results may differ from the reference program's by a relative error of at most 0.0003.
Values sent between devices are 32-bit elements; how exact they have to be, the bound alone decides.
No kernel may reach another device: no remote copies, remote signals or barrier semaphores. Data moves between devices by JAX's collectives and lax.ppermute only.
A program may use at most 64 MiB of HBM per device.

```python
import jax
import jax.numpy as jnp
from jax import lax

ORDER = 65536
BS = 512
VEC = 128
NB = 2
FILTER_DEG = 2
TILE_ROWS = 32
TILE_COLS = 16
N_ROW = 4
N_COL = 8


def tile_positions(key):
    cell_total = TILE_ROWS * TILE_COLS
    scores = jax.random.randint(key, (N_ROW * N_COL, cell_total), 0, 1 << 20)
    scores = scores * cell_total + jnp.arange(cell_total, dtype=jnp.int32)[None, :]
    chosen = jnp.argsort(scores, axis=-1, stable=True)[:, :NB].astype(jnp.int32)
    return chosen.reshape(N_ROW, N_COL * NB)


def draw_block_rows(key, part):
    return (tile_positions(jax.random.fold_in(key, 7)) // TILE_COLS).astype(jnp.int32)


def draw_block_cols(key, part):
    return (tile_positions(jax.random.fold_in(key, 7)) % TILE_COLS).astype(jnp.int32)


def draw_block_count(key, part):
    key_list = jax.random.split(jax.random.fold_in(key, 13), 3)
    first_draw = jax.random.randint(key_list[0], (N_ROW * N_COL,), 0, NB)
    second_draw = jax.random.randint(key_list[1], (N_ROW * N_COL,), 0, NB)
    counts = jnp.minimum(first_draw, second_draw) + 1
    busiest = jax.random.randint(key_list[2], (), 0, N_ROW * N_COL)
    counts = jnp.where(jnp.arange(N_ROW * N_COL) == busiest, NB, counts)
    return counts.reshape(N_ROW, N_COL).astype(jnp.int32)


def levels(own_key, dims, cuts, low, top_value):
    gain, own = 1.0, jax.random.fold_in(own_key, 6)
    for position, parts in cuts:
        draws = jnp.exp(jax.random.uniform(jax.random.fold_in(own, position), (parts,), jnp.float32, low / len(cuts), top_value / len(cuts)))
        gain = gain * jnp.repeat(draws, dims[position] // parts).reshape([-1 if axis == position else 1 for axis in range(len(dims))])
    return gain


def scatter_about(key, dims, spread, limit, cuts=(), held_as=jnp.bfloat16):
    drawn = jax.random.normal(key, dims, jnp.float32) * spread
    if len(cuts) > 0:
        drawn = levels(key, dims, cuts, -0.22, 0.18) * drawn
    return jnp.clip(drawn, min=-limit, max=limit).astype(held_as)


def setup_inputs(seed: int = 0) -> dict:
    key_of = jax.random.split(jax.random.key(seed), 8)
    start_block = scatter_about(key_of[0], (ORDER, VEC), 1.0, 6.0, ((0, 32),), jnp.float32)
    block_values = scatter_about(key_of[1], (N_ROW, N_COL * NB, BS, BS), (BS * max(1, NB * N_COL // TILE_ROWS)) ** -0.5, 0.25, ((0, 4), (1, 8)), jnp.float32)
    block_rows = draw_block_rows(jax.random.fold_in(key_of[7], 71), 0)
    block_cols = draw_block_cols(jax.random.fold_in(key_of[7], 71), 0)
    block_count = draw_block_count(jax.random.fold_in(key_of[7], 71), 0)
    center = jnp.clip(jax.random.uniform(key_of[5], (1,), jnp.float32, 0.5, 1.0), 0.5, 1.0)
    radius = jnp.clip(jax.random.uniform(key_of[6], (1,), jnp.float32, 0.8, 1.2), 0.8, 1.2)
    return {"start_block": start_block, "block_values": block_values, "block_rows": block_rows, "block_cols": block_cols, "block_count": block_count, "center": center, "radius": radius}


HIGHEST_PRECISION = lax.Precision.HIGHEST

def half_product(vectors, block_values, block_rows, block_cols, block_count, transpose):
    vec_blocks = vectors.reshape(ORDER // BS, BS, VEC)
    slot_rank = jnp.arange(N_COL * NB, dtype=jnp.int32)
    group_ids = (slot_rank // NB).astype(jnp.int32)
    slot_within = (slot_rank % NB).astype(jnp.int32)

    def per_row(running, inputs):
        values, rows_here, cols_here, counts_here, row_group = inputs
        row_ids = (row_group * TILE_ROWS + rows_here).astype(jnp.int32)
        col_ids = (group_ids * TILE_COLS + cols_here).astype(jnp.int32)
        live_mask = (slot_within < counts_here[group_ids]).astype(jnp.float32)
        if transpose:
            picked = vec_blocks[row_ids]
            products = jnp.einsum('sba,sbv->sav', values, picked, precision=HIGHEST_PRECISION)
            products = products * live_mask[:, None, None]
            running = running + jax.ops.segment_sum(products, col_ids, ORDER // BS)
        else:
            picked = vec_blocks[col_ids]
            products = jnp.einsum('sab,sbv->sav', values, picked, precision=HIGHEST_PRECISION)
            products = products * live_mask[:, None, None]
            running = running + jax.ops.segment_sum(products, row_ids, ORDER // BS)
        return (running, None)
    zeros_start = jnp.zeros((ORDER // BS, BS, VEC), jnp.float32)
    inputs = (block_values, block_rows, block_cols, block_count, jnp.arange(N_ROW, dtype=jnp.int32))
    running, unused = lax.scan(per_row, zeros_start, inputs)
    return running.reshape(ORDER, VEC)

def reference(start_block, block_values, block_rows, block_cols, block_count, center, radius):

    def apply_scaled(vectors):
        middle = half_product(vectors, block_values, block_rows, block_cols, block_count, True)
        system = half_product(middle, block_values, block_rows, block_cols, block_count, False)
        return (system - center[0] * vectors) / radius[0]
    previous = start_block
    current = apply_scaled(start_block)
    for degree_step in range(FILTER_DEG - 1):
        following = 2.0 * apply_scaled(current) - previous
        previous = current
        current = following
    gram_matrix = jnp.dot(current.T, current, precision=HIGHEST_PRECISION)
    lower_factor = jnp.linalg.cholesky(gram_matrix)
    basis_block = jax.scipy.linalg.solve_triangular(lower_factor, current.T, lower=True).T
    image_block = half_product(basis_block, block_values, block_rows, block_cols, block_count, True)
    projected = jnp.dot(image_block.T, image_block, precision=HIGHEST_PRECISION)
    return (basis_block, projected)
```

```python
import functools

import jax
import jax.numpy as jnp
import numpy as np
from jax import lax
from jax.experimental import pallas as pl
from jax.experimental.pallas import tpu as pltpu
from jax.sharding import PartitionSpec as P

HIGHEST = lax.Precision.HIGHEST
HALVES = 2
VMEM = pl.BlockSpec(memory_space=pltpu.VMEM)
SMEM = pl.BlockSpec(memory_space=pltpu.SMEM)
ANY = pl.BlockSpec(memory_space=pl.ANY)


def call(kernel, out_shape, in_specs, out_specs, args, scratch=(), flops=0, name=None):
    moved = sum(a.size * a.dtype.itemsize for a in args)
    return pl.pallas_call(
        kernel,
        out_shape=out_shape,
        in_specs=in_specs,
        out_specs=out_specs,
        scratch_shapes=list(scratch),
        compiler_params=pltpu.CompilerParams(vmem_limit_bytes=40 * 1024 * 1024),
        cost_estimate=pl.CostEstimate(flops=flops, bytes_accessed=moved, transcendentals=0),
        name=name,
    )(*args)


def unpack(packed):
    width = packed.shape[-1] // HALVES
    return jnp.concatenate([packed[:, i * width : (i + 1) * width] for i in range(HALVES)], axis=0)


def pack(block):
    rows = block.shape[0] // HALVES
    return jnp.concatenate([block[i * rows : (i + 1) * rows] for i in range(HALVES)], axis=1)


def split(value):
    high = value.astype(jnp.bfloat16)
    return high, (value - high.astype(jnp.float32)).astype(jnp.bfloat16)


def dot3(left_high, left_low, right):
    right_high, right_low = split(right)
    dot = functools.partial(jnp.dot, preferred_element_type=jnp.float32)
    return dot(left_high, right_high) + (dot(left_high, right_low) + dot(left_low, right_high))


def prepare_kernel(values, high, low, high_t, low_t):
    for s in range(values.shape[0]):
        block = values[s]
        high[s], low[s] = split(block)
        high_t[s], low_t[s] = split(block.T)


class Own:
    def __init__(self, start, first_piece, half):
        self.start, self.first, self.half = start, first_piece, half

    def pick(self, row, other):
        piece, vec = other.shape
        width = vec // HALVES
        held = self.start.shape[0] // piece
        lane = lax.broadcasted_iota(jnp.int32, other.shape, 1) // width
        parts, mask = [], None
        for i in range(HALVES):
            local = row * HALVES + i - self.first
            valid = (row >= 0) & (local >= 0) & (local < held)
            at = pl.multiple_of(jnp.clip(local, 0, held - 1) * piece, piece)
            rows = self.start[pl.ds(at, piece), :]
            parts.append(rows[:, self.half * width : (self.half + 1) * width])
            here = (lane == i) & valid
            mask = here if mask is None else mask | here
        return jnp.where(mask, jnp.concatenate(parts, axis=1), other)


def table_row(table, places, entry, slots, slot):
    place = places[entry]
    return jnp.where(place >= 0, table[jnp.maximum(place, 0) * slots + slot], -1)


def y_kernel(entries, half, slots, table, places, start, *outs):
    own = Own(start, places[0], half)
    for entry, out in zip(entries, outs):
        for s in range(slots):
            row = table_row(table, places, entry, slots, s)
            out[s] = own.pick(row, jnp.zeros(out.shape[1:], out.dtype))


def z_kernel(up_entry, down_entry, half, slots, has_second, has_before, table, places, start, *refs):
    refs = list(refs)
    up_out, down_out = refs[-2:]
    first = refs.pop(0)
    second = refs.pop(0) if has_second else None
    below, above = refs[:2] if has_before else (None, None)
    own = Own(start, places[0], half)
    up_there = places[up_entry] >= 0
    for s in range(slots):
        base_up = first[s]
        base_down = jnp.where(up_there, second[s], first[s]) if has_second else first[s]
        if has_before:
            base_up, base_down = base_up + below[s], base_down + above[s]
        up_out[s] = own.pick(table_row(table, places, up_entry, slots, s), base_up)
        down_out[s] = own.pick(table_row(table, places, down_entry, slots, s), base_down)


def first_kernel(half, slots, own_entry, table, places, start, high_t, low_t, *refs):
    arrived, (x_out, p_out) = refs[:-2], refs[-2:]
    own = Own(start, places[0], half)
    for s in range(slots):
        base = arrived[0][s]
        for more in arrived[1:]:
            base = base + more[s]
        x = own.pick(table_row(table, places, own_entry, slots, s), base)
        x_out[s] = x
        p_out[s] = pack(dot3(high_t[s], low_t[s], unpack(x)))


def add_columns(columns, arrived, slots, total):
    for s in range(slots):
        mine = columns[s]
        total[s] = arrived[0][s]
        for j, held in enumerate(arrived):
            for t in range(slots):
                if (j, t) != (0, s):

                    @pl.when((columns[j * slots + t] == mine) & (mine >= 0))
                    def _():
                        total[s] += held[t]


def column_kernel(slots, columns, high, low, *refs):
    arrived, q_out, total = refs[:-2], refs[-2], refs[-1]
    add_columns(columns, arrived, slots, total)
    for s in range(slots):
        q_out[s] = pack(dot3(high[s], low[s], unpack(total[s])))


def row_kernel(slots, entries, order, table, places, scalars, high_t, low_t, mine, vectors, older, *refs):
    count = len(entries)
    arrived = refs[:count]
    y_out, p_out, total, landing, sems = refs[count:]
    center, radius = scalars[0], scalars[1]

    def each(action):
        for b, entry in enumerate(entries):
            for t in range(slots):
                row = table_row(table, places, entry, slots, t)
                hit = row < -1
                for s in range(slots):
                    hit = hit | ((row == table[s]) & (row >= 0))

                @pl.when(hit)
                def _():
                    action(b, t, row)

    def copy(b, t):
        return pltpu.make_async_copy(arrived[b].at[t], landing.at[b * slots + t], sems.at[b * slots + t])

    each(lambda b, t, row: copy(b, t).start())
    for s in range(slots):
        total[s] = mine[s]
        for t in range(slots):
            if t != s:

                @pl.when((table[t] == table[s]) & (table[s] >= 0))
                def _():
                    total[s] += mine[t]

    def add(b, t, row):
        copy(b, t).wait()
        for s in range(slots):

            @pl.when(row == table[s])
            def _():
                total[s] += landing[b * slots + t]

    each(add)
    for s in range(slots):
        y = (total[s] - center * vectors[s]) / radius
        if order == 2:
            y = 2.0 * y - older[s]
        y_out[s] = y
        p_out[s] = pack(dot3(high_t[s], low_t[s], unpack(y)))


def owner_kernel(slots, entries, order, table, places, scalars, current, older, *refs):
    count = len(entries)
    arrived = [refs[h * count : (h + 1) * count] for h in range(HALVES)]
    refs = refs[HALVES * count :]
    y_out = refs[0]
    gram_out = refs[1] if order == 2 else None
    landing, sems = refs[-2:]
    center, radius = scalars[0], scalars[1]
    piece, vec = landing.shape[1:]
    width = vec // HALVES
    held = y_out.shape[0] // piece
    first = places[0]

    def each(action):
        for b, entry in enumerate(entries):
            for t in range(slots):
                row = table_row(table, places, entry, slots, t)
                begin = row * HALVES - first
                hit = (row >= 0) & (begin + HALVES > 0) & (begin < held)

                @pl.when(hit)
                def _():
                    for h in range(HALVES):
                        action(h, b, t, begin)

    def copy(h, b, t):
        at = (h * count + b) * slots + t
        return pltpu.make_async_copy(arrived[h][b].at[t], landing.at[at], sems.at[at])

    each(lambda h, b, t, begin: copy(h, b, t).start())
    y_out[...] = jnp.zeros(y_out.shape, y_out.dtype)

    def add(h, b, t, begin):
        copy(h, b, t).wait()
        block = landing[(h * count + b) * slots + t]
        for i in range(HALVES):
            local = begin + i

            @pl.when((local >= 0) & (local < held))
            def _():
                at = pl.multiple_of(jnp.clip(local, 0, held - 1) * piece, piece)
                part = block[:, i * width : (i + 1) * width]
                y_out[pl.ds(at, piece), h * width : (h + 1) * width] += part

    each(add)
    y = (y_out[...] - center * current[...]) / radius
    if order == 2:
        y = 2.0 * y - older[...]
        y_out[...] = y
        gram_out[...] = lax.dot_general(
            y, y, (((0,), (0,)), ((), ())), precision=HIGHEST, preferred_element_type=jnp.float32
        )
    else:
        y_out[...] = y


def inner_kernel(slots, rows, columns, *refs):
    refs = list(refs)
    out, total, left, right = refs[-4:]
    arrived = [refs[h * rows : (h + 1) * rows] for h in range(HALVES)]
    for h in range(HALVES):
        add_columns(columns, arrived[h], slots, total)
        for s in range(slots):
            piece, vec = total.shape[1:]
            width = vec // HALVES
            for i in range(HALVES):
                at = (s * HALVES + i) * piece
                left[at : at + piece, h * width : (h + 1) * width] = arrived[h][0][s][:, i * width : (i + 1) * width]
                right[at : at + piece, h * width : (h + 1) * width] = total[s][:, i * width : (i + 1) * width]
    out[...] = lax.dot_general(
        left[...], right[...], (((0,), (0,)), ((), ())), precision=HIGHEST, preferred_element_type=jnp.float32
    )


def solution(mesh):
    n_row, n_col = mesh.shape["row"], mesh.shape["col"]
    pair = 2 if n_col % 2 == 0 else 1
    line = n_col // pair

    names, lines = {"first": 0}, [[0] for _ in range(n_col)]

    def entry(name, place):
        names[name] = len(lines[0])
        for col in range(n_col):
            z, y = col // pair, col % pair
            there = place(z, y)
            lines[col].append(-1 if there is None or not 0 <= there[0] < line else col ^ (there[0] * pair + there[1]))

    def primary(step):
        return lambda z, y: (z + step, 1 - y) if z + step < line else (z - step, 1 - y)

    def secondary(step):
        return lambda z, y: (z - step, 1 - y) if z + step < line else None

    entry("own", lambda z, y: (z, y))
    for step in range(line):
        entry(f"first{step}", primary(step))
        entry(f"second{step}", secondary(step))
        entry(f"up{step}", lambda z, y: (z + step, y))
        entry(f"down{step}", lambda z, y: (z - step, y))
        entry(f"other_up{step}", lambda z, y: (z + step, 1 - y))
        entry(f"other_down{step}", lambda z, y: (z - step, 1 - y))
    place_lines = np.array(lines, np.int32)

    def over(flag):
        return [z for z in range(line) if flag(z)]

    def up(value, zs):
        pairs = [(z * pair + y, (z + 1) * pair + y) for z in zs for y in range(pair)]
        return lax.ppermute(value, "col", pairs)

    def down(value, zs):
        pairs = [(z * pair + y, (z - 1) * pair + y) for z in zs for y in range(pair)]
        return lax.ppermute(value, "col", pairs)

    def across(value, zs):
        return lax.ppermute(value, "col", [(z * pair + y, z * pair + 1 - y) for z in zs for y in range(pair)])

    def exclusive(value, axis, bit):
        size = n_row if axis == "row" else n_col
        return lax.ppermute(value, axis, [(i, i ^ bit) for i in range(size)])

    def table_of(own, axis):
        size = n_row if axis == "row" else n_col
        return jnp.concatenate([own] + [exclusive(own, axis, j) for j in range(1, size)])

    def gather_row(own):
        held = {0: own}
        bit = n_row // 2
        while bit:
            held.update({j ^ bit: exclusive(v, "row", bit) for j, v in list(held.items())})
            bit //= 2
        return [held[j] for j in range(n_row)]

    def sum_all(value):
        for axis, size in (("row", n_row), ("col", n_col)):
            bit = 1
            while bit < size:
                value = value + exclusive(value, axis, bit)
                bit *= 2
        return value

    def gather_entries():
        entries = []
        for step in range(1, line):
            entries += [names[f"down{step}"], names[f"up{step}"]]
        if pair == 2:
            entries.append(names["other_up0"])
            for step in range(1, line):
                entries += [names[f"other_down{step}"], names[f"other_up{step}"]]
        return entries

    def gather_col(own):
        same, other = [], [across(own, range(line))] if pair == 2 else []
        below = above = own
        for step in range(1, line):
            below = up(below, over(lambda z: z - step + 1 >= 0 and z + 1 < line))
            above = down(above, over(lambda z: z + step - 1 < line and z >= 1))
            same += [below, above]
            if pair == 2:
                other.append(across(below, over(lambda z: z - step >= 0)))
                other.append(across(above, over(lambda z: z + step < line)))
        return same + other

    def body(start_block, block_values, block_rows, block_cols, block_count, center, radius):
        values = block_values[0]
        slots, size, _ = values.shape
        held_rows, vec = start_block.shape
        piece = size // HALVES
        live = jnp.arange(slots) < block_count[0, 0]
        rows = jnp.where(live, block_rows[0], -1)
        cols = jnp.where(live, block_cols[0], -1)
        col = lax.axis_index("col")
        with jax.named_scope("tables"):
            table = table_of(rows, "col")
            columns = table_of(cols, "row")
        places = jnp.asarray(place_lines)[col]
        places = places.at[0].set(col * (held_rows // piece))
        scalars = jnp.concatenate([center, radius])

        chunk = jax.ShapeDtypeStruct((slots, piece, vec), jnp.float32)
        half_block = jax.ShapeDtypeStruct(values.shape, jnp.bfloat16)
        high, low, high_t, low_t = call(
            prepare_kernel, [half_block] * 4, [VMEM], [VMEM] * 4, [values], name="split_blocks"
        )
        flops = 6 * slots * size * size * (vec // HALVES)

        def pick_start(half):
            sends, arrived = [], {}
            if pair == 2:
                wanted = []
                for step in range(line - 1, -1, -1):
                    zs = over(lambda z: z + step < line or z - step >= 0)
                    if zs:
                        wanted.append((f"first{step}", zs))
                    zs = over(lambda z: z + step < line and z - step >= 0)
                    if zs and step:
                        wanted.append((f"second{step}", zs))
                sends = call(
                    functools.partial(y_kernel, [names[n] for n, _ in wanted], half, slots),
                    [chunk] * len(wanted),
                    [SMEM, SMEM, VMEM],
                    [VMEM] * len(wanted),
                    [table, places, start_block],
                    name="pick_other",
                )
                for (n, zs), value in zip(wanted, sends):
                    arrived[n] = across(value, zs)
            else:
                arrived = {f"first{step}": jnp.zeros(chunk.shape, chunk.dtype) for step in range(line)}
            below = above = None
            for step in range(line - 1, 0, -1):
                got = [arrived[f"first{step}"]]
                has_second = f"second{step}" in arrived
                if has_second:
                    got.append(arrived[f"second{step}"])
                if below is not None:
                    got += [below, above]
                up_part, down_part = call(
                    functools.partial(
                        z_kernel, names[f"up{step}"], names[f"down{step}"], half, slots, has_second, below is not None
                    ),
                    [chunk] * 2,
                    [SMEM, SMEM, VMEM] + [VMEM] * len(got),
                    [VMEM] * 2,
                    [table, places, start_block] + got,
                    name="pick_line",
                )
                below = up(up_part, over(lambda z: z + step < line))
                above = down(down_part, over(lambda z: z - step >= 0))
            got = [arrived["first0"]] + ([below, above] if below is not None else [])
            return call(
                functools.partial(first_kernel, half, slots, names["own"]),
                [chunk] * 2,
                [SMEM, SMEM] + [VMEM] * (3 + len(got)),
                [VMEM] * 2,
                [table, places, start_block, high_t, low_t] + got,
                flops=flops,
                name="first_product",
            )

        def column_step(parts):
            return call(
                functools.partial(column_kernel, slots),
                chunk,
                [SMEM] + [VMEM] * (2 + n_row),
                VMEM,
                [columns, high, low] + parts,
                scratch=[pltpu.VMEM(chunk.shape, jnp.float32)],
                flops=flops,
                name="column_product",
            )

        entries = gather_entries()
        count = len(entries)

        def row_step(order, mine, got, vectors, older):
            return call(
                functools.partial(row_kernel, slots, entries, order),
                [chunk] * 2,
                [SMEM] * 3 + [VMEM] * 5 + [ANY] * count,
                [VMEM] * 2,
                [table, places, scalars, high_t, low_t, mine, vectors, older] + got,
                scratch=[
                    pltpu.VMEM(chunk.shape, jnp.float32),
                    pltpu.VMEM((count * slots, piece, vec), jnp.float32),
                    pltpu.SemaphoreType.DMA((count * slots,)),
                ],
                flops=flops,
                name="row_product",
            )

        owner_entries = [names["own"]] + entries
        everything = HALVES * (count + 1) * slots

        def owner_step(order, current, older, got):
            dense = jax.ShapeDtypeStruct(start_block.shape, jnp.float32)
            gram = [jax.ShapeDtypeStruct((vec, vec), jnp.float32)] if order == 2 else []
            return call(
                functools.partial(owner_kernel, slots, owner_entries, order),
                [dense] + gram,
                [SMEM] * 3 + [VMEM] * 2 + [ANY] * (HALVES * (count + 1)),
                [VMEM] * (1 + len(gram)),
                [table, places, scalars, current, older] + sum(got, []),
                scratch=[
                    pltpu.VMEM((everything, piece, vec), jnp.float32),
                    pltpu.SemaphoreType.DMA((everything,)),
                ],
                flops=0 if order == 1 else 2 * held_rows * vec * vec,
                name="owner_rows",
            )

        first_sums, second_sums, images = [], [], []
        state = [pick_start(half) for half in range(HALVES)]
        for half in range(HALVES):
            x, p = state[half]
            q = column_step(gather_row(p))
            got = gather_col(q)
            first_sums.append([q] + got)
            y, p = row_step(1, q, got, x, x)
            q = column_step(gather_row(p))
            got = gather_col(q)
            second_sums.append([q] + got)
            _, p = row_step(2, q, got, y, x)
            images.append(gather_row(p))

        (current,) = owner_step(1, start_block, start_block, first_sums)
        following, gram_local = owner_step(2, current, start_block, second_sums)
        inner_local = call(
            functools.partial(inner_kernel, slots, n_row),
            jax.ShapeDtypeStruct((vec, vec), jnp.float32),
            [SMEM] + [VMEM] * (HALVES * n_row),
            VMEM,
            [columns] + sum(images, []),
            scratch=[
                pltpu.VMEM(chunk.shape, jnp.float32),
                pltpu.VMEM((slots * size, vec), jnp.float32),
                pltpu.VMEM((slots * size, vec), jnp.float32),
            ],
            name="inner_product",
        )
        gram_matrix = sum_all(gram_local)
        inner_matrix = sum_all(inner_local)
        lower_factor = jnp.linalg.cholesky(gram_matrix)
        basis_block = jax.scipy.linalg.solve_triangular(lower_factor, following.T, lower=True).T
        left_solved = jax.scipy.linalg.solve_triangular(lower_factor, inner_matrix, lower=True)
        projected = jax.scipy.linalg.solve_triangular(lower_factor, left_solved.T, lower=True).T
        return (basis_block, projected)

    in_specs = (
        P(("row", "col"), None),
        P("row", "col", None, None),
        P("row", "col"),
        P("row", "col"),
        P("row", "col"),
        P(),
        P(),
    )
    out_specs = (P(("row", "col"), None), P())
    return jax.shard_map(body, mesh=mesh, in_specs=in_specs, out_specs=out_specs, check_vma=False)
```

```python
import functools

import jax
import jax.numpy as jnp
import numpy as np
from jax import lax
from jax.experimental import pallas as pl
from jax.experimental.pallas import tpu as pltpu
from jax.sharding import PartitionSpec as P

HIGHEST = lax.Precision.HIGHEST
PANEL = 8
VMEM = pl.BlockSpec(memory_space=pltpu.VMEM)
SMEM = pl.BlockSpec(memory_space=pltpu.SMEM)
ANY = pl.BlockSpec(memory_space=pl.ANY)


def call(kernel, out_shape, in_specs, out_specs, args, scratch=(), flops=0, name=None):
    moved = sum(a.size * a.dtype.itemsize for a in args)
    return pl.pallas_call(
        kernel,
        out_shape=out_shape,
        in_specs=in_specs,
        out_specs=out_specs,
        scratch_shapes=list(scratch),
        compiler_params=pltpu.CompilerParams(vmem_limit_bytes=40 * 1024 * 1024),
        cost_estimate=pl.CostEstimate(flops=flops, bytes_accessed=moved, transcendentals=0),
        name=name,
    )(*args)


def split(value):
    high = value.astype(jnp.bfloat16)
    return high, (value - high.astype(jnp.float32)).astype(jnp.bfloat16)


def dot3(left_high, left_low, right):
    right_high, right_low = split(right)
    dot = functools.partial(jnp.dot, preferred_element_type=jnp.float32)
    return dot(left_high, right_high) + (dot(left_high, right_low) + dot(left_low, right_high))


def self_product(value):
    high, low = split(value)

    def dot(left, right):
        return lax.dot_general(left, right, (((0,), (0,)), ((), ())), preferred_element_type=jnp.float32)

    mixed = dot(high, low)
    return dot(high, high) + (dot(low, low) + (mixed + mixed.T))


def prepare_kernel(values, high, low, high_t, low_t):
    for s in range(values.shape[0]):
        block = values[s]
        high[s], low[s] = split(block)
        high_t[s], low_t[s] = split(block.T)


def table_row(table, places, entry, slots, slot):
    place = places[entry]
    return jnp.where(place >= 0, table[jnp.maximum(place, 0) * slots + slot], -1)


def pick(row, held, first, piece, out, s, base):
    size = out.shape[1]
    count = held.shape[0] // piece
    for i in range(size // piece):
        rows = slice(i * piece, (i + 1) * piece)
        value = jnp.zeros((piece, out.shape[2]), out.dtype)
        for ref, slot in base:
            value = value + ref[slot, rows, :]
        local = row * (size // piece) + i - first
        valid = (row >= 0) & (local >= 0) & (local < count)
        at = pl.multiple_of(jnp.clip(local, 0, count - 1) * piece, piece)
        out[s, rows, :] = jnp.where(valid, held[pl.ds(at, piece), :], value)


def ring_kernel(entry, slots, offset, before_offset, piece, table, places, held, *refs):
    before, out = refs[:-1], refs[-1]
    for s in range(out.shape[0]):
        slot = s + offset
        base = [(ref, slot - before_offset) for ref in before if 0 <= slot - before_offset < ref.shape[0]]
        pick(table_row(table, places, entry, slots, slot), held, places[0], piece, out, s, base)


def first_kernel(entry, slots, offsets, piece, table, places, held, high_t, low_t, *refs):
    arrived, (x_out, p_out) = refs[:-2], refs[-2:]
    for s in range(slots):
        base = [(ref, s - off) for ref, off in zip(arrived, offsets) if 0 <= s - off < ref.shape[0]]
        pick(table_row(table, places, entry, slots, s), held, places[0], piece, x_out, s, base)
        p_out[s] = dot3(high_t[s], low_t[s], x_out[s])


def column_kernel(slots, last, columns, scalars, high, low, *refs):
    refs = list(refs)
    older = refs.pop(0) if last else None
    arrived, q_out, total = refs[:-2], refs[-2], refs[-1]
    center, radius = scalars[0], scalars[1]
    for s in range(slots):
        mine = columns[s]
        total[s] = arrived[0][s]
        for j, held in enumerate(arrived):
            for t in range(slots):
                if (j, t) != (0, s):

                    @pl.when((columns[j * slots + t] == mine) & (mine >= 0))
                    def _():
                        total[s] += held[t]

        q = dot3(high[s], low[s], total[s])
        if last:
            q = (2.0 / radius) * (q - (center / radius) * older[s])
        q_out[s] = q


def row_kernel(slots, entries, last, table, places, scalars, high_t, low_t, mine, vectors, *refs):
    count = len(entries)
    arrived = refs[:count]
    p_out, total, landing, sems = refs[count:]
    center, radius = scalars[0], scalars[1]

    def each(action):
        for b, (entry, offset) in enumerate(entries):
            for t in range(arrived[b].shape[0]):
                row = table_row(table, places, entry, slots, offset + t)
                hit = row < -1
                for s in range(slots):
                    hit = hit | ((row == table[s]) & (row >= 0))

                @pl.when(hit)
                def _():
                    action(b, t, row)

    def copy(b, t):
        return pltpu.make_async_copy(arrived[b].at[t], landing.at[b * slots + t], sems.at[b * slots + t])

    each(lambda b, t, row: copy(b, t).start())
    for s in range(slots):
        total[s] = mine[s]
        for t in range(slots):
            if t != s:

                @pl.when((table[t] == table[s]) & (table[s] >= 0))
                def _():
                    total[s] += mine[t]

    def add(b, t, row):
        copy(b, t).wait()
        for s in range(slots):

            @pl.when(row == table[s])
            def _():
                total[s] += landing[b * slots + t]

    each(add)
    for s in range(slots):
        if last:
            y = total[s] + (2.0 * (center / radius) * (center / radius) - 1.0) * vectors[s]
        else:
            y = (total[s] - center * vectors[s]) / radius
        p_out[s] = dot3(high_t[s], low_t[s], y)


def owner_kernel(slots, entries, piece, table, places, scalars, start, *refs):
    count = len(entries)
    arrived = refs[:count]
    y_out, gram_out, landing, sems = refs[count:]
    center, radius = scalars[0], scalars[1]
    subs = landing.shape[1] // piece
    held = y_out.shape[0] // piece
    first = places[0]

    def each(action):
        for b, (entry, offset) in enumerate(entries):
            for t in range(arrived[b].shape[0]):
                row = table_row(table, places, entry, slots, offset + t)
                begin = row * subs - first

                @pl.when((row >= 0) & (begin + subs > 0) & (begin < held))
                def _():
                    action(b, t, begin)

    def copy(b, t):
        return pltpu.make_async_copy(arrived[b].at[t], landing.at[b * slots + t], sems.at[b * slots + t])

    each(lambda b, t, begin: copy(b, t).start())
    y_out[...] = (2.0 * (center / radius) * (center / radius) - 1.0) * start[...]

    def add(b, t, begin):
        copy(b, t).wait()
        for i in range(subs):
            local = begin + i

            @pl.when((local >= 0) & (local < held))
            def _():
                at = pl.multiple_of(jnp.clip(local, 0, held - 1) * piece, piece)
                y_out[pl.ds(at, piece), :] += landing[b * slots + t, i * piece : (i + 1) * piece, :]

    each(add)
    gram_out[...] = self_product(y_out[...])


def inner_kernel(slots, columns, place, *refs):
    arrived, out, order, total = refs[:-3], refs[-3], refs[-2], refs[-1]
    count = len(arrived)
    size = order.shape[1]
    for j, held in enumerate(arrived):
        at = lax.bitwise_xor(place[0], j)
        for t in range(slots):
            order[at * slots + t] = held[t]

    def column(i):
        return columns[lax.bitwise_xor(place[0], i // slots) * slots + i % slots]

    ids = [column(i) for i in range(count * slots)]
    for i in range(count * slots):
        earlier = ids[i] < 0
        for k in range(i):
            earlier = earlier | (ids[k] == ids[i])
        total[i * size : (i + 1) * size, :] = jnp.where(earlier, 0.0, order[i])
        for k in range(i + 1, count * slots):

            @pl.when((ids[k] == ids[i]) & jnp.logical_not(earlier))
            def _():
                total[i * size : (i + 1) * size, :] += order[k]

    out[...] = self_product(total[...])


def factor_kernel(gram, following, basis_out, inverse_out):
    order = gram.shape[0]
    blocks = order // PANEL
    shape = (PANEL, order)
    below = lax.broadcasted_iota(jnp.int32, shape, 0)
    lane = lax.broadcasted_iota(jnp.int32, shape, 1)
    left = [gram[b * PANEL : (b + 1) * PANEL, :] for b in range(blocks)]
    right = [jnp.where(lane == below + b * PANEL, 1.0, 0.0) for b in range(blocks)]

    def spread(block, k):
        return jnp.broadcast_to(block[k : k + 1, :], shape)

    for b in range(blocks):
        rest = range(b, blocks)
        panel = [
            {i: jnp.broadcast_to(left[i][:, b * PANEL + j : b * PANEL + j + 1], shape) for i in rest}
            for j in range(PANEL)
        ]
        scale = jnp.ones(shape, jnp.float32)
        for k in range(PANEL):
            pivot = spread(panel[k][b], k)
            inverse = 1.0 / pivot
            scale = jnp.where(below == k, lax.rsqrt(pivot), scale)
            factor = {i: panel[k][i] * inverse for i in rest}
            factor[b] = jnp.where(below > k, factor[b], 0.0)
            left_row, right_row = spread(left[b], k), spread(right[b], k)
            for j in range(k + 1, PANEL):
                row = spread(panel[j][b], k)
                for i in rest:
                    panel[j][i] = panel[j][i] - factor[i] * row
            for i in rest:
                left[i] = left[i] - factor[i] * left_row
                right[i] = right[i] - factor[i] * right_row
        inverse_out[b * PANEL : (b + 1) * PANEL, :] = right[b] * scale
    basis_out[...] = lax.dot_general(
        following[...], inverse_out[...], (((1,), (1,)), ((), ())), precision=HIGHEST, preferred_element_type=jnp.float32
    )


def project_kernel(inverse, inner, out):
    half = jnp.dot(inverse[...], inner[...], precision=HIGHEST, preferred_element_type=jnp.float32)
    out[...] = lax.dot_general(
        half, inverse[...], (((1,), (1,)), ((), ())), precision=HIGHEST, preferred_element_type=jnp.float32
    )


def solution(mesh):
    n_row, n_col = mesh.shape["row"], mesh.shape["col"]
    tie = lax.optimization_barrier
    far = n_col // 2

    ring = list(range(0, n_col, 2)) + list(range(1, n_col, 2))[::-1]
    position = {col: k for k, col in enumerate(ring)}

    place_lines = np.array(
        [[0] + [col ^ ring[(position[col] + d) % n_col] for d in range(-far, far + 1)] for col in range(n_col)], np.int32
    )

    def at(distance):
        return far + 1 + distance

    def forward(value, step):
        return lax.ppermute(value, "col", [(col, ring[(k + step) % n_col]) for k, col in enumerate(ring)])

    def shares(distance, slots):
        if 2 * distance < n_col:
            return (0, slots), (0, slots)
        if slots % 2:
            return (0, slots), (0, 0)
        return (0, slots // 2), (slots // 2, slots)

    def flip(value, axis, bit):
        size = n_row if axis == "row" else n_col
        return lax.ppermute(value, axis, [(i, i ^ bit) for i in range(size)])

    def table_over(own, axis):
        for bit in powers(n_row if axis == "row" else n_col):
            own = jnp.concatenate([own, flip(own, axis, bit)])
        return own

    def gather_row(own):
        held = {0: own}
        bit = n_row // 2
        while bit:
            held.update({j ^ bit: flip(v, "row", bit) for j, v in list(held.items())})
            bit //= 2
        return [held[j] for j in range(n_row)]

    def sum_over(value, axis, bits):
        for bit in bits:
            value = value + flip(value, axis, bit)
        return value

    def powers(size):
        return [1 << k for k in range(size.bit_length() - 1)]

    def gather_col(own):
        slots = own.shape[0]
        held = {1: (own, 0), -1: (own, 0)}
        got = []
        for distance in range(1, far + 1):
            for step, (first, end) in zip((1, -1), shares(distance, slots)):
                if first == end:
                    continue
                chunk, _ = held[step]
                if (first, end) != (0, slots):
                    chunk = chunk[first:end]
                held[step] = (forward(chunk, step), first)
                got.append(((at(-step * distance), first), held[step][0]))
        return [g[0] for g in got], [g[1] for g in got]

    def body(start_block, block_values, block_rows, block_cols, block_count, center, radius):
        values = block_values[0]
        slots, size, _ = values.shape
        held_rows, vec = start_block.shape
        piece = min(size, held_rows)
        live = jnp.arange(slots) < block_count[0, 0]
        rows = jnp.where(live, block_rows[0], -1)
        cols = jnp.where(live, block_cols[0], -1)
        col = lax.axis_index("col")
        with jax.named_scope("tables"):
            table = table_over(rows, "col")
            columns = table_over(cols, "row")
        places = jnp.asarray(place_lines)[col]
        held_pieces = held_rows // piece
        places = places.at[0].set(col * held_pieces)
        scalars = jnp.concatenate([center, radius])

        chunk = jax.ShapeDtypeStruct((slots, size, vec), jnp.float32)
        square = jax.ShapeDtypeStruct((vec, vec), jnp.float32)
        half_block = jax.ShapeDtypeStruct(values.shape, jnp.bfloat16)
        high, low, high_t, low_t = call(
            prepare_kernel, [half_block] * 4, [VMEM], [VMEM] * 4, [values], name="split_blocks"
        )
        flops = 6 * slots * size * size * vec

        before = {1: [], -1: []}
        for distance in range(far, 0, -1):
            for step, (first, end) in zip((1, -1), shares(distance, slots)):
                if first == end:
                    continue
                value = call(
                    functools.partial(
                        ring_kernel, at(step * distance), slots, first, sum(b[1] for b in before[step]), piece
                    ),
                    jax.ShapeDtypeStruct((end - first, size, vec), jnp.float32),
                    [SMEM, SMEM] + [VMEM] * (1 + len(before[step])),
                    VMEM,
                    [table, places, start_block] + [b[0] for b in before[step]],
                    name="pick_rows",
                )
                before[step] = [(forward(value, step), first)]
            if distance == 2:
                (first_value, offset) = before[1][0]
                first_value, columns, high, low, high_t, low_t = tie((first_value, columns, high, low, high_t, low_t))
                before[1] = [(first_value, offset)]
        arrived = before[1] + before[-1]
        x, p = call(
            functools.partial(first_kernel, at(0), slots, [b[1] for b in arrived], piece),
            [chunk] * 2,
            [SMEM, SMEM] + [VMEM] * (3 + len(arrived)),
            [VMEM] * 2,
            [table, places, start_block, high_t, low_t] + [b[0] for b in arrived],
            flops=flops,
            name="first_product",
        )

        def column_step(parts, older=None):
            more = [] if older is None else [older]
            return call(
                functools.partial(column_kernel, slots, older is not None),
                chunk,
                [SMEM, SMEM] + [VMEM] * (2 + len(more) + n_row),
                VMEM,
                [columns, scalars, high, low] + more + parts,
                scratch=[pltpu.VMEM(chunk.shape, jnp.float32)],
                flops=flops,
                name="column_product",
            )

        def row_step(last, mine, entries, got, vectors):
            count = len(got)
            return call(
                functools.partial(row_kernel, slots, entries, last),
                chunk,
                [SMEM] * 3 + [VMEM] * 4 + [ANY] * count,
                VMEM,
                [table, places, scalars, high_t, low_t, mine, vectors] + got,
                scratch=[
                    pltpu.VMEM(chunk.shape, jnp.float32),
                    pltpu.VMEM((count * slots, size, vec), jnp.float32),
                    pltpu.SemaphoreType.DMA((count * slots,)),
                ],
                flops=flops,
                name="row_product",
            )

        q = column_step(gather_row(p))
        p = row_step(False, q, *gather_col(q), x)
        g = column_step(gather_row(p), q)
        entries, got = gather_col(g)
        count = len(got)

        following, gram_local = call(
            functools.partial(owner_kernel, slots, [(at(0), 0)] + entries, piece),
            [jax.ShapeDtypeStruct(start_block.shape, jnp.float32), square],
            [SMEM] * 3 + [VMEM] + [ANY] * (count + 1),
            [VMEM] * 2,
            [table, places, scalars, start_block, g] + got,
            scratch=[
                pltpu.VMEM(((count + 1) * slots, size, vec), jnp.float32),
                pltpu.SemaphoreType.DMA(((count + 1) * slots,)),
            ],
            flops=6 * held_rows * vec * vec,
            name="owner_rows",
        )
        gram_matrix, g = tie((gram_local, g))
        p = row_step(True, g, entries, got, x)
        gram_matrix = sum_over(gram_matrix, "row", powers(n_row)[:1])
        gram_matrix = sum_over(gram_matrix, "col", powers(n_col))
        gram_matrix = sum_over(gram_matrix, "row", powers(n_row)[1:])
        inner_local = call(
            functools.partial(inner_kernel, slots),
            square,
            [SMEM, SMEM] + [VMEM] * n_row,
            VMEM,
            [columns, lax.axis_index("row").reshape(1)] + gather_row(p),
            scratch=[
                pltpu.VMEM((n_row * slots, size, vec), jnp.float32),
                pltpu.VMEM((n_row * slots * size, vec), jnp.float32),
            ],
            flops=6 * n_row * slots * size * vec * vec,
            name="inner_product",
        )
        inner_matrix = sum_over(inner_local, "col", powers(n_col))
        basis_block, inverse = call(
            factor_kernel,
            [jax.ShapeDtypeStruct(start_block.shape, jnp.float32), square],
            [VMEM] * 2,
            [VMEM] * 2,
            [gram_matrix, following],
            flops=12 * held_rows * vec * vec,
            name="factor_and_basis",
        )
        projected = call(project_kernel, square, [VMEM] * 2, VMEM, [inverse, inner_matrix], name="project")
        return (basis_block, projected)

    in_specs = (
        P(("row", "col"), None),
        P("row", "col", None, None),
        P("row", "col"),
        P("row", "col"),
        P("row", "col"),
        P(),
        P(),
    )
    out_specs = (P(("row", "col"), None), P())
    return jax.shard_map(body, mesh=mesh, in_specs=in_specs, out_specs=out_specs, check_vma=False)
```

```python
import functools

import jax
import jax.numpy as jnp
import numpy as np
from jax import lax
from jax.experimental import pallas as pl
from jax.experimental.pallas import tpu as pltpu
from jax.sharding import PartitionSpec as P

HIGHEST = lax.Precision.HIGHEST
PANEL = 8
VMEM = pl.BlockSpec(memory_space=pltpu.VMEM)
SMEM = pl.BlockSpec(memory_space=pltpu.SMEM)
ANY = pl.BlockSpec(memory_space=pl.ANY)


def call(kernel, out_shape, in_specs, out_specs, args, scratch=(), flops=0, name=None):
    moved = sum(a.size * a.dtype.itemsize for a in args)
    return pl.pallas_call(
        kernel,
        out_shape=out_shape,
        in_specs=in_specs,
        out_specs=out_specs,
        scratch_shapes=list(scratch),
        compiler_params=pltpu.CompilerParams(vmem_limit_bytes=40 * 1024 * 1024),
        cost_estimate=pl.CostEstimate(flops=flops, bytes_accessed=moved, transcendentals=0),
        name=name,
    )(*args)


def split(value):
    high = value.astype(jnp.bfloat16)
    return high, (value - high.astype(jnp.float32)).astype(jnp.bfloat16)


def dot3(left_high, left_low, right):
    right_high, right_low = split(right)
    dot = functools.partial(jnp.dot, preferred_element_type=jnp.float32)
    return dot(left_high, right_high) + (dot(left_high, right_low) + dot(left_low, right_high))


def self_product(value):
    high, low = split(value)

    def dot(left, right):
        return lax.dot_general(left, right, (((0,), (0,)), ((), ())), preferred_element_type=jnp.float32)

    mixed = dot(high, low)
    return dot(high, high) + (dot(low, low) + (mixed + mixed.T))


def prepare_kernel(slots, values, *outs):
    for s in range(slots):
        high, low, high_t, low_t = outs[4 * s : 4 * s + 4]
        high[...], low[...] = split(values[s])
        high_t[...], low_t[...] = split(values[s].T)


def table_row(table, places, entry, slots, slot):
    place = places[entry]
    return jnp.where(place >= 0, table[jnp.maximum(place, 0) * slots + slot], -1)


def pick(row, held, first_unit, unit, per_block, out, begin, base):
    vec = out.shape[1]
    count = held.shape[0] // unit
    for i in range(out.shape[0] // unit):
        value = jnp.zeros((unit, vec), out.dtype)
        for ref, ref_begin in base:
            at = begin + i * unit - ref_begin
            if 0 <= at < ref.shape[0]:
                value = value + ref[at : at + unit, :]
        local = row * per_block + begin // unit + i - first_unit
        valid = (row >= 0) & (local >= 0) & (local < count)
        rows = pl.ds(pl.multiple_of(jnp.clip(local, 0, count - 1) * unit, unit), unit)
        out[i * unit : (i + 1) * unit, :] = jnp.where(valid, held[rows, :], value)


def ring_kernel(entry, slots, slot, begin, befores, unit, per_block, table, places, held, *refs):
    base, out = list(zip(refs[:-1], befores)), refs[-1]
    pick(table_row(table, places, entry, slots, slot), held, places[0], unit, per_block, out, begin, base)


def first_kernel(entry, slots, slot, befores, unit, per_block, table, places, held, high_t, low_t, *refs):
    base, (x_out, p_out) = list(zip(refs[:-2], befores)), refs[-2:]
    pick(table_row(table, places, entry, slots, slot), held, places[0], unit, per_block, x_out, 0, base)
    p_out[...] = dot3(high_t[...], low_t[...], x_out[...])


def add_matching(hits, copies, total):
    for hit, (copy, _, _) in zip(hits, copies):

        @pl.when(hit)
        def _():
            copy.start()

    for hit, (copy, landing, rows) in zip(hits, copies):

        @pl.when(hit)
        def _():
            copy.wait()
            total[rows, :] += landing[...]


def column_kernel(slots, slot, last, columns, scalars, high, low, *refs):
    refs = list(refs)
    older = refs.pop(0) if last else None
    mine = refs.pop(0)
    arrived, (q_out, total, landing, sems) = refs[:-4], refs[-4:]
    center, radius = scalars[0], scalars[1]
    column = columns[slot]
    others = [k for k in range(len(arrived) + 1) if k != slot]
    hits, copies = [], []
    for i, k in enumerate(others):
        hits.append((columns[k] == column) & (column >= 0))
        copies.append(
            (pltpu.make_async_copy(arrived[i], landing.at[i], sems.at[i]), landing.at[i], slice(0, total.shape[0]))
        )
    total[...] = mine[...]
    add_matching(hits, copies, total)
    q = dot3(high[...], low[...], total[...])
    if last:
        q = (2.0 / radius) * (q - (center / radius) * older[...])
    q_out[...] = q


def row_kernel(slots, pieces, last, table, places, scalars, *refs):
    refs = list(refs)
    high_t, low_t, mine, vectors = [[refs.pop(0) for _ in range(slots)] for _ in range(4)]
    arrived, p_out, (total, landing, sems) = refs[: len(pieces)], refs[len(pieces) : -3], refs[-3:]
    center, radius = scalars[0], scalars[1]
    rows = [table_row(table, places, entry, slots, slot) for entry, slot, _ in pieces]

    def copy(b):
        return pltpu.make_async_copy(arrived[b], landing.at[b, pl.ds(0, arrived[b].shape[0])], sems.at[b])

    def each(action):
        for b in range(len(pieces)):
            hit = rows[b] < -1
            for s in range(slots):
                hit = hit | ((rows[b] == table[s]) & (rows[b] >= 0))

            @pl.when(hit)
            def _():
                action(b)

    each(lambda b: copy(b).start())
    for s in range(slots):
        total[s] = mine[s][...]
        for t in range(slots):
            if t != s:

                @pl.when((table[t] == table[s]) & (table[s] >= 0))
                def _():
                    total[s] += mine[t][...]

    def add(b):
        copy(b).wait()
        first, count = pieces[b][2], arrived[b].shape[0]
        for s in range(slots):

            @pl.when(rows[b] == table[s])
            def _():
                total[s, first : first + count, :] += landing[b, :count, :]

    each(add)
    for s in range(slots):
        if last:
            y = total[s] + (2.0 * (center / radius) * (center / radius) - 1.0) * vectors[s][...]
        else:
            y = (total[s] - center * vectors[s][...]) / radius
        p_out[s][...] = dot3(high_t[s][...], low_t[s][...], y)


def owner_kernel(slots, pieces, unit, per_block, table, places, scalars, start, *refs):
    arrived, (y_out, gram_out, landing, sems) = refs[:-4], refs[-4:]
    center, radius = scalars[0], scalars[1]
    held = y_out.shape[0] // unit

    def copy(b):
        return pltpu.make_async_copy(arrived[b], landing.at[b, pl.ds(0, arrived[b].shape[0])], sems.at[b])

    def each(action):
        for b, (entry, slot, first) in enumerate(pieces):
            row = table_row(table, places, entry, slots, slot)
            count = arrived[b].shape[0] // unit
            begin = row * per_block + first // unit - places[0]

            @pl.when((row >= 0) & (begin + count > 0) & (begin < held))
            def _():
                action(b, begin, count)

    each(lambda b, begin, count: copy(b).start())
    y_out[...] = (2.0 * (center / radius) * (center / radius) - 1.0) * start[...]

    def add(b, begin, count):
        copy(b).wait()
        for i in range(count):
            local = begin + i

            @pl.when((local >= 0) & (local < held))
            def _():
                rows = pl.ds(pl.multiple_of(jnp.clip(local, 0, held - 1) * unit, unit), unit)
                y_out[rows, :] += landing[b, i * unit : (i + 1) * unit, :]

    each(add)
    gram_out[...] = self_product(y_out[...])


def inner_kernel(slots, columns, place, *refs):
    arrived, out, order, total = refs[:-3], refs[-3], refs[-2], refs[-1]
    count, size = len(arrived), order.shape[1]
    for k, held in enumerate(arrived):
        order[lax.bitwise_xor(place[0], k // slots) * slots + k % slots] = held[...]
    ids = [columns[lax.bitwise_xor(place[0], i // slots) * slots + i % slots] for i in range(count)]
    for i in range(count):
        earlier = ids[i] < 0
        for k in range(i):
            earlier = earlier | (ids[k] == ids[i])
        total[i * size : (i + 1) * size, :] = jnp.where(earlier, 0.0, order[i])
        for k in range(i + 1, count):

            @pl.when((ids[k] == ids[i]) & jnp.logical_not(earlier))
            def _():
                total[i * size : (i + 1) * size, :] += order[k]

    out[...] = self_product(total[...])


def factor_kernel(gram, following, basis_out, inverse_out):
    order = gram.shape[0]
    blocks = order // PANEL
    shape = (PANEL, order)
    below = lax.broadcasted_iota(jnp.int32, shape, 0)
    lane = lax.broadcasted_iota(jnp.int32, shape, 1)
    left = [gram[b * PANEL : (b + 1) * PANEL, :] for b in range(blocks)]
    right = [jnp.where(lane == below + b * PANEL, 1.0, 0.0) for b in range(blocks)]

    def spread(block, k):
        return jnp.broadcast_to(block[k : k + 1, :], shape)

    for b in range(blocks):
        rest = range(b, blocks)
        panel = [
            {i: jnp.broadcast_to(left[i][:, b * PANEL + j : b * PANEL + j + 1], shape) for i in rest}
            for j in range(PANEL)
        ]
        scale = jnp.ones(shape, jnp.float32)
        for k in range(PANEL):
            pivot = spread(panel[k][b], k)
            inverse = 1.0 / pivot
            scale = jnp.where(below == k, lax.rsqrt(pivot), scale)
            factor = {i: panel[k][i] * inverse for i in rest}
            factor[b] = jnp.where(below > k, factor[b], 0.0)
            left_row, right_row = spread(left[b], k), spread(right[b], k)
            for j in range(k + 1, PANEL):
                row = spread(panel[j][b], k)
                for i in rest:
                    panel[j][i] = panel[j][i] - factor[i] * row
            for i in rest:
                left[i] = left[i] - factor[i] * left_row
                right[i] = right[i] - factor[i] * right_row
        inverse_out[b * PANEL : (b + 1) * PANEL, :] = right[b] * scale
    basis_out[...] = lax.dot_general(
        following[...], inverse_out[...], (((1,), (1,)), ((), ())), precision=HIGHEST, preferred_element_type=jnp.float32
    )


def project_kernel(inverse, inner, out):
    half = jnp.dot(inverse[...], inner[...], precision=HIGHEST, preferred_element_type=jnp.float32)
    out[...] = lax.dot_general(
        half, inverse[...], (((1,), (1,)), ((), ())), precision=HIGHEST, preferred_element_type=jnp.float32
    )


def solution(mesh):
    n_row, n_col = mesh.shape["row"], mesh.shape["col"]
    tie = lax.optimization_barrier
    far = n_col // 2

    ring = list(range(0, n_col, 2)) + list(range(1, n_col, 2))[::-1]
    position = {col: k for k, col in enumerate(ring)}

    place_lines = np.array(
        [[0] + [col ^ ring[(position[col] + d) % n_col] for d in range(-far, far + 1)] for col in range(n_col)], np.int32
    )

    def at(distance):
        return far + 1 + distance

    def forward(value, step):
        return lax.ppermute(value, "col", [(col, ring[(k + step) % n_col]) for k, col in enumerate(ring)])

    def shares(distance, size):
        if 2 * distance < n_col:
            return (1, 0, size), (-1, 0, size)
        return (1, 0, size // 2), (-1, size // 2, size)

    def flip(value, axis, bit):
        size = n_row if axis == "row" else n_col
        return lax.ppermute(value, axis, [(i, i ^ bit) for i in range(size)])

    def table_over(own, axis):
        for bit in powers(n_row if axis == "row" else n_col):
            own = jnp.concatenate([own, flip(own, axis, bit)])
        return own

    def gather_rest(own, across):
        top = powers(n_row)[-1]
        held = {0: own, top: across}
        bit = top // 2
        while bit:
            held.update({j ^ bit: [flip(v, "row", bit) for v in values] for j, values in list(held.items())})
            bit //= 2
        return sum([held[j] for j in range(n_row)], [])

    def gather_row(own):
        return gather_rest(own, [flip(value, "row", powers(n_row)[-1]) for value in own])

    def sum_over(value, axis, bits):
        for bit in bits:
            value = value + flip(value, axis, bit)
        return value

    def powers(size):
        return [1 << k for k in range(size.bit_length() - 1)]

    def gather_col(own):
        held = [{1: value, -1: value} for value in own]
        pieces, got = [], []
        for distance in range(1, far + 1):
            for slot, value in enumerate(own):
                for step, first, end in shares(distance, value.shape[0]):
                    chunk = held[slot][step]
                    if end - first < chunk.shape[0]:
                        chunk = chunk[first:end]
                    held[slot][step] = forward(chunk, step)
                    pieces.append((at(-step * distance), slot, first))
                    got.append(held[slot][step])
        return pieces, got

    def body(start_block, block_values, block_rows, block_cols, block_count, center, radius):
        values = block_values[0]
        slots, size, _ = values.shape
        held_rows, vec = start_block.shape
        unit = min(size // 2, held_rows)
        per_block = size // unit
        live = jnp.arange(slots) < block_count[0, 0]
        rows = jnp.where(live, block_rows[0], -1)
        cols = jnp.where(live, block_cols[0], -1)
        col = lax.axis_index("col")
        with jax.named_scope("tables"):
            table = table_over(rows, "col")
            columns = table_over(cols, "row")
        places = jnp.asarray(place_lines)[col]
        places = places.at[0].set(col * (held_rows // unit))
        scalars = jnp.concatenate([center, radius])
        row_bits, col_bits = powers(n_row), powers(n_col)

        chunk = jax.ShapeDtypeStruct((size, vec), jnp.float32)
        square = jax.ShapeDtypeStruct((vec, vec), jnp.float32)
        half_block = jax.ShapeDtypeStruct((size, size), jnp.bfloat16)
        blocks = call(
            functools.partial(prepare_kernel, slots),
            [half_block] * (4 * slots),
            [VMEM],
            [VMEM] * (4 * slots),
            [values],
            name="split_blocks",
        )
        flops = 6 * size * size * vec

        before = [{1: [], -1: []} for _ in range(slots)]
        for distance in range(far, 0, -1):
            for slot in range(slots):
                for step, first, end in shares(distance, size):
                    prior = before[slot][step]
                    value = call(
                        functools.partial(
                            ring_kernel, at(step * distance), slots, slot, first, [b[1] for b in prior], unit, per_block
                        ),
                        jax.ShapeDtypeStruct((end - first, vec), jnp.float32),
                        [SMEM, SMEM] + [VMEM] * (1 + len(prior)),
                        VMEM,
                        [table, places, start_block] + [b[0] for b in prior],
                        name="pick_rows",
                    )
                    before[slot][step] = [(forward(value, step), first)]
            if distance == 2:
                value, first = before[0][1][0]
                value, columns, blocks = tie((value, columns, blocks))
                before[0][1] = [(value, first)]
        high, low, high_t, low_t = [[blocks[4 * s + k] for s in range(slots)] for k in range(4)]

        def first_step(slot):
            arrived = before[slot][1] + before[slot][-1]
            return call(
                functools.partial(first_kernel, at(0), slots, slot, [b[1] for b in arrived], unit, per_block),
                [chunk] * 2,
                [SMEM, SMEM] + [VMEM] * (3 + len(arrived)),
                [VMEM] * 2,
                [table, places, start_block, high_t[slot], low_t[slot]] + [b[0] for b in arrived],
                flops=flops,
                name="first_product",
            )

        def column_step(chunks, older=None):
            out = []
            for slot in range(slots):
                others = chunks[:slot] + chunks[slot + 1 :]
                more = [] if older is None else [older[slot]]
                out.append(
                    call(
                        functools.partial(column_kernel, slots, slot, older is not None),
                        chunk,
                        [SMEM, SMEM] + [VMEM] * (3 + len(more)) + [ANY] * len(others),
                        VMEM,
                        [columns, scalars, high[slot], low[slot]] + more + [chunks[slot]] + others,
                        scratch=[
                            pltpu.VMEM(chunk.shape, jnp.float32),
                            pltpu.VMEM((len(others), size, vec), jnp.float32),
                            pltpu.SemaphoreType.DMA((len(others),)),
                        ],
                        flops=flops,
                        name="column_product",
                    )
                )
            return out

        def row_step(last, mine, pieces, got, vectors):
            return call(
                functools.partial(row_kernel, slots, pieces, last),
                [chunk] * slots,
                [SMEM] * 3 + [VMEM] * (4 * slots) + [ANY] * len(got),
                [VMEM] * slots,
                [table, places, scalars] + high_t + low_t + mine + vectors + got,
                scratch=[
                    pltpu.VMEM((slots, size, vec), jnp.float32),
                    pltpu.VMEM((len(got), size, vec), jnp.float32),
                    pltpu.SemaphoreType.DMA((len(got),)),
                ],
                flops=flops * slots,
                name="row_product",
            )

        xs, ps = zip(*[first_step(slot) for slot in range(slots)])
        xs, ps = list(xs), list(ps)
        qs = column_step(gather_row(ps))
        ps = list(row_step(False, qs, *gather_col(qs), xs))
        gs = column_step(gather_row(ps), qs)
        pieces, got = gather_col(gs)

        owner_pieces = [(at(0), slot, 0) for slot in range(slots)] + pieces
        following, gram_matrix = call(
            functools.partial(owner_kernel, slots, owner_pieces, unit, per_block),
            [jax.ShapeDtypeStruct(start_block.shape, jnp.float32), square],
            [SMEM] * 3 + [VMEM] + [ANY] * len(owner_pieces),
            [VMEM] * 2,
            [table, places, scalars, start_block] + gs + got,
            scratch=[
                pltpu.VMEM((len(owner_pieces), size, vec), jnp.float32),
                pltpu.SemaphoreType.DMA((len(owner_pieces),)),
            ],
            flops=6 * held_rows * vec * vec,
            name="owner_rows",
        )
        gram_matrix, gs = tie((gram_matrix, gs))
        ps = list(row_step(True, gs, pieces, got, xs))
        gram_matrix = sum_over(gram_matrix, "row", row_bits[:-1])
        across = [flip(p, "row", row_bits[-1]) for p in ps]
        gram_matrix = sum_over(gram_matrix, "col", col_bits[:2])
        gram_matrix, across = tie((gram_matrix, across))
        images = gather_rest(ps, across)
        gram_matrix = sum_over(gram_matrix, "col", col_bits[2:])
        gram_matrix = sum_over(gram_matrix, "row", row_bits[-1:])
        inner_local = call(
            functools.partial(inner_kernel, slots),
            square,
            [SMEM, SMEM] + [VMEM] * len(images),
            VMEM,
            [columns, lax.axis_index("row").reshape(1)] + images,
            scratch=[
                pltpu.VMEM((len(images), size, vec), jnp.float32),
                pltpu.VMEM((len(images) * size, vec), jnp.float32),
            ],
            flops=6 * len(images) * size * vec * vec,
            name="inner_product",
        )
        inner_matrix = sum_over(inner_local, "col", col_bits)
        basis_block, inverse = call(
            factor_kernel,
            [jax.ShapeDtypeStruct(start_block.shape, jnp.float32), square],
            [VMEM] * 2,
            [VMEM] * 2,
            [gram_matrix, following],
            flops=12 * held_rows * vec * vec,
            name="factor_and_basis",
        )
        projected = call(project_kernel, square, [VMEM] * 2, VMEM, [inverse, inner_matrix], name="project")
        return (basis_block, projected)

    in_specs = (
        P(("row", "col"), None),
        P("row", "col", None, None),
        P("row", "col"),
        P("row", "col"),
        P("row", "col"),
        P(),
        P(),
    )
    out_specs = (P(("row", "col"), None), P())
    return jax.shard_map(body, mesh=mesh, in_specs=in_specs, out_specs=out_specs, check_vma=False)
```

```python
import functools

import jax
import jax.numpy as jnp
import numpy as np
from jax import lax
from jax.experimental import pallas as pl
from jax.experimental.pallas import tpu as pltpu
from jax.sharding import PartitionSpec as P

HIGHEST = lax.Precision.HIGHEST
PANEL = 8
VMEM = pl.BlockSpec(memory_space=pltpu.VMEM)
SMEM = pl.BlockSpec(memory_space=pltpu.SMEM)
ANY = pl.BlockSpec(memory_space=pl.ANY)


def call(kernel, out_shape, in_specs, out_specs, args, scratch=(), flops=0, name=None):
    moved = sum(a.size * a.dtype.itemsize for a in args)
    return pl.pallas_call(
        kernel,
        out_shape=out_shape,
        in_specs=in_specs,
        out_specs=out_specs,
        scratch_shapes=list(scratch),
        compiler_params=pltpu.CompilerParams(vmem_limit_bytes=40 * 1024 * 1024),
        cost_estimate=pl.CostEstimate(flops=flops, bytes_accessed=moved, transcendentals=0),
        name=name,
    )(*args)


def split(value):
    high = value.astype(jnp.bfloat16)
    return high, (value - high.astype(jnp.float32)).astype(jnp.bfloat16)


def dot3(left_high, left_low, right):
    right_high, right_low = split(right)
    dot = functools.partial(jnp.dot, preferred_element_type=jnp.float32)
    return dot(left_high, right_high) + (dot(left_high, right_low) + dot(left_low, right_high))


def self_product(value):
    high, low = split(value)

    def dot(left, right):
        return lax.dot_general(left, right, (((0,), (0,)), ((), ())), preferred_element_type=jnp.float32)

    mixed = dot(high, low)
    return dot(high, high) + (dot(low, low) + (mixed + mixed.T))


def prepare_kernel(slots, values, *outs):
    for s in range(slots):
        high, low, high_t, low_t = outs[4 * s : 4 * s + 4]
        high[...], low[...] = split(values[s])
        high_t[...], low_t[...] = split(values[s].T)


def table_row(table, places, entry, slots, slot):
    return table[places[entry] * slots + slot]


def pick(row, held, first_unit, unit, per_block, out, begin, base):
    vec = out.shape[1]
    count = held.shape[0] // unit
    for i in range(out.shape[0] // unit):
        value = jnp.zeros((unit, vec), out.dtype)
        for ref, ref_begin in base:
            at = begin + i * unit - ref_begin
            if 0 <= at < ref.shape[0]:
                value = value + ref[at : at + unit, :]
        local = row * per_block + begin // unit + i - first_unit
        valid = (row >= 0) & (local >= 0) & (local < count)
        rows = pl.ds(pl.multiple_of(jnp.clip(local, 0, count - 1) * unit, unit), unit)
        out[i * unit : (i + 1) * unit, :] = jnp.where(valid, held[rows, :], value)


def ring_kernel(entry, slots, slot, begin, befores, unit, per_block, table, places, held, *refs):
    base, out = list(zip(refs[:-1], befores)), refs[-1]
    pick(table_row(table, places, entry, slots, slot), held, places[0], unit, per_block, out, begin, base)


def first_kernel(entry, slots, slot, befores, unit, per_block, table, places, held, high_t, low_t, *refs):
    base, (x_out, p_out) = list(zip(refs[:-2], befores)), refs[-2:]
    pick(table_row(table, places, entry, slots, slot), held, places[0], unit, per_block, x_out, 0, base)
    p_out[...] = dot3(high_t[...], low_t[...], x_out[...])


def add_matching(hits, copies, total):
    for hit, (copy, _, _) in zip(hits, copies):

        @pl.when(hit)
        def _():
            copy.start()

    for hit, (copy, landing, rows) in zip(hits, copies):

        @pl.when(hit)
        def _():
            copy.wait()
            total[rows, :] += landing[...]


def column_kernel(slots, slot, last, columns, scalars, high, low, *refs):
    refs = list(refs)
    older = refs.pop(0) if last else None
    mine = refs.pop(0)
    arrived, (q_out, total, landing, sems) = refs[:-4], refs[-4:]
    center, radius = scalars[0], scalars[1]
    column = columns[slot]
    others = [k for k in range(len(arrived) + 1) if k != slot]
    hits, copies = [], []
    for i, k in enumerate(others):
        hits.append((columns[k] == column) & (column >= 0))
        copies.append(
            (pltpu.make_async_copy(arrived[i], landing.at[i], sems.at[i]), landing.at[i], slice(0, total.shape[0]))
        )
    total[...] = mine[...]
    add_matching(hits, copies, total)
    q = dot3(high[...], low[...], total[...])
    if last:
        q = (2.0 / radius) * (q - (center / radius) * older[...])
    q_out[...] = q


def row_kernel(slots, pieces, last, table, places, scalars, *refs):
    refs = list(refs)
    high_t, low_t, mine, vectors = [[refs.pop(0) for _ in range(slots)] for _ in range(4)]
    arrived, p_out, (total, landing, sems) = refs[: len(pieces)], refs[len(pieces) : -3], refs[-3:]
    center, radius = scalars[0], scalars[1]
    rows = [table_row(table, places, entry, slots, slot) for entry, slot, _ in pieces]

    def copy(b):
        return pltpu.make_async_copy(arrived[b], landing.at[b, pl.ds(0, arrived[b].shape[0])], sems.at[b])

    def each(action):
        for b in range(len(pieces)):
            hit = rows[b] < -1
            for s in range(slots):
                hit = hit | ((rows[b] == table[s]) & (rows[b] >= 0))

            @pl.when(hit)
            def _():
                action(b)

    each(lambda b: copy(b).start())
    for s in range(slots):
        total[s] = mine[s][...]
        for t in range(slots):
            if t != s:

                @pl.when((table[t] == table[s]) & (table[s] >= 0))
                def _():
                    total[s] += mine[t][...]

    def add(b):
        copy(b).wait()
        first, count = pieces[b][2], arrived[b].shape[0]
        for s in range(slots):

            @pl.when(rows[b] == table[s])
            def _():
                total[s, first : first + count, :] += landing[b, :count, :]

    each(add)
    for s in range(slots):
        if last:
            y = total[s] + (2.0 * (center / radius) * (center / radius) - 1.0) * vectors[s][...]
        else:
            y = (total[s] - center * vectors[s][...]) / radius
        p_out[s][...] = dot3(high_t[s][...], low_t[s][...], y)


def owner_kernel(slots, pieces, unit, per_block, table, places, scalars, start, *refs):
    arrived, (y_out, gram_out, landing, sems) = refs[:-4], refs[-4:]
    center, radius = scalars[0], scalars[1]
    held = y_out.shape[0] // unit

    def copy(b):
        return pltpu.make_async_copy(arrived[b], landing.at[b, pl.ds(0, arrived[b].shape[0])], sems.at[b])

    def each(action):
        for b, (entry, slot, first) in enumerate(pieces):
            row = table_row(table, places, entry, slots, slot)
            count = arrived[b].shape[0] // unit
            begin = row * per_block + first // unit - places[0]

            @pl.when((row >= 0) & (begin + count > 0) & (begin < held))
            def _():
                action(b, begin, count)

    each(lambda b, begin, count: copy(b).start())
    y_out[...] = (2.0 * (center / radius) * (center / radius) - 1.0) * start[...]

    def add(b, begin, count):
        copy(b).wait()
        for i in range(count):
            local = begin + i

            @pl.when((local >= 0) & (local < held))
            def _():
                rows = pl.ds(pl.multiple_of(jnp.clip(local, 0, held - 1) * unit, unit), unit)
                y_out[rows, :] += landing[b, i * unit : (i + 1) * unit, :]

    each(add)
    gram_out[...] = self_product(y_out[...])


def inner_kernel(slots, columns, place, *refs):
    arrived, out, order, total = refs[:-3], refs[-3], refs[-2], refs[-1]
    count, size = len(arrived), order.shape[1]
    for k, held in enumerate(arrived):
        order[lax.bitwise_xor(place[0], k // slots) * slots + k % slots] = held[...]
    ids = [columns[lax.bitwise_xor(place[0], i // slots) * slots + i % slots] for i in range(count)]
    for i in range(count):
        earlier = ids[i] < 0
        for k in range(i):
            earlier = earlier | (ids[k] == ids[i])
        total[i * size : (i + 1) * size, :] = jnp.where(earlier, 0.0, order[i])
        for k in range(i + 1, count):

            @pl.when((ids[k] == ids[i]) & jnp.logical_not(earlier))
            def _():
                total[i * size : (i + 1) * size, :] += order[k]

    out[...] = self_product(total[...])


def factor_kernel(gram, inverse_out):
    order = gram.shape[0]
    blocks = order // PANEL
    shape = (PANEL, order)
    below = lax.broadcasted_iota(jnp.int32, shape, 0)
    lane = lax.broadcasted_iota(jnp.int32, shape, 1)
    left = [gram[b * PANEL : (b + 1) * PANEL, :] for b in range(blocks)]
    right = [jnp.where(lane == below + b * PANEL, 1.0, 0.0) for b in range(blocks)]

    def spread(block, k):
        return jnp.broadcast_to(block[k : k + 1, :], shape)

    for b in range(blocks):
        rest = range(b, blocks)
        panel = [
            {i: jnp.broadcast_to(left[i][:, b * PANEL + j : b * PANEL + j + 1], shape) for i in rest}
            for j in range(PANEL)
        ]
        scale = jnp.ones(shape, jnp.float32)
        for k in range(PANEL):
            pivot = spread(panel[k][b], k)
            inverse = 1.0 / pivot
            scale = jnp.where(below == k, lax.rsqrt(pivot), scale)
            factor = {i: panel[k][i] * inverse for i in rest}
            factor[b] = jnp.where(below > k, factor[b], 0.0)
            left_row, right_row = spread(left[b], k), spread(right[b], k)
            for j in range(k + 1, PANEL):
                row = spread(panel[j][b], k)
                for i in rest:
                    panel[j][i] = panel[j][i] - factor[i] * row
            for i in rest:
                left[i] = left[i] - factor[i] * left_row
                right[i] = right[i] - factor[i] * right_row
        inverse_out[b * PANEL : (b + 1) * PANEL, :] = right[b] * scale


def basis_kernel(following, inverse, out):
    out[...] = lax.dot_general(
        following[...], inverse[...], (((1,), (1,)), ((), ())), precision=HIGHEST, preferred_element_type=jnp.float32
    )


def project_kernel(inverse, inner, out):
    half = jnp.dot(inverse[...], inner[...], precision=HIGHEST, preferred_element_type=jnp.float32)
    out[...] = lax.dot_general(
        half, inverse[...], (((1,), (1,)), ((), ())), precision=HIGHEST, preferred_element_type=jnp.float32
    )


def solution(mesh):
    n_row, n_col = mesh.shape["row"], mesh.shape["col"]
    tie = lax.optimization_barrier
    far = n_col // 2

    ring = list(range(0, n_col, 2)) + list(range(1, n_col, 2))[::-1]
    position = {col: k for k, col in enumerate(ring)}

    place_lines = np.array(
        [[0] + [col ^ ring[(position[col] + d) % n_col] for d in range(-far, far + 1)] for col in range(n_col)], np.int32
    )

    def at(distance):
        return far + 1 + distance

    def forward(value, step):
        return lax.ppermute(value, "col", [(col, ring[(k + step) % n_col]) for k, col in enumerate(ring)])

    def shares(distance, size):
        if 2 * distance < n_col:
            return (1, 0, size), (-1, 0, size)
        return (1, 0, size // 2), (-1, size // 2, size)

    def flip(value, axis, bit):
        size = n_row if axis == "row" else n_col
        return lax.ppermute(value, axis, [(i, i ^ bit) for i in range(size)])

    def table_over(own, axis):
        for bit in powers(n_row if axis == "row" else n_col):
            own = jnp.concatenate([own, flip(own, axis, bit)])
        return own

    def gather_rest(own, across):
        top = powers(n_row)[-1]
        held = {0: own, top: across}
        bit = top // 2
        while bit:
            held.update({j ^ bit: [flip(v, "row", bit) for v in values] for j, values in list(held.items())})
            bit //= 2
        return sum([held[j] for j in range(n_row)], [])

    def gather_row(own):
        return gather_rest(own, [flip(value, "row", powers(n_row)[-1]) for value in own])

    def sum_over(value, axis, bits):
        for bit in bits:
            value = value + flip(value, axis, bit)
        return value

    def powers(size):
        return [1 << k for k in range(size.bit_length() - 1)]

    def gather_col(own):
        held = [{1: value, -1: value} for value in own]
        pieces, got = [], []
        for distance in range(1, far + 1):
            for slot, value in enumerate(own):
                for step, first, end in shares(distance, value.shape[0]):
                    chunk = held[slot][step]
                    if end - first < chunk.shape[0]:
                        chunk = chunk[first:end]
                    held[slot][step] = forward(chunk, step)
                    pieces.append((at(-step * distance), slot, first))
                    got.append(held[slot][step])
        return pieces, got

    def body(start_block, block_values, block_rows, block_cols, block_count, center, radius):
        values = block_values[0]
        slots, size, _ = values.shape
        held_rows, vec = start_block.shape
        unit = min(size // 2, held_rows)
        per_block = size // unit
        live = jnp.arange(slots) < block_count[0, 0]
        rows = jnp.where(live, block_rows[0], -1)
        cols = jnp.where(live, block_cols[0], -1)
        col = lax.axis_index("col")
        with jax.named_scope("tables"):
            table = table_over(rows, "col")
            columns = table_over(cols, "row")
        places = jnp.asarray(place_lines)[col]
        places = places.at[0].set(col * (held_rows // unit))
        scalars = jnp.concatenate([center, radius])
        row_bits, col_bits = powers(n_row), powers(n_col)

        chunk = jax.ShapeDtypeStruct((size, vec), jnp.float32)
        square = jax.ShapeDtypeStruct((vec, vec), jnp.float32)
        half_block = jax.ShapeDtypeStruct((size, size), jnp.bfloat16)
        blocks = call(
            functools.partial(prepare_kernel, slots),
            [half_block] * (4 * slots),
            [VMEM],
            [VMEM] * (4 * slots),
            [values],
            name="split_blocks",
        )
        flops = 6 * size * size * vec

        before = [{1: [], -1: []} for _ in range(slots)]
        for distance in range(far, 0, -1):
            for slot in range(slots):
                for step, first, end in shares(distance, size):
                    prior = before[slot][step]
                    value = call(
                        functools.partial(
                            ring_kernel, at(step * distance), slots, slot, first, [b[1] for b in prior], unit, per_block
                        ),
                        jax.ShapeDtypeStruct((end - first, vec), jnp.float32),
                        [SMEM, SMEM] + [VMEM] * (1 + len(prior)),
                        VMEM,
                        [table, places, start_block] + [b[0] for b in prior],
                        name="pick_rows",
                    )
                    before[slot][step] = [(forward(value, step), first)]
            if distance == 2:
                value, first = before[0][1][0]
                value, columns, blocks = tie((value, columns, blocks))
                before[0][1] = [(value, first)]
        high, low, high_t, low_t = [[blocks[4 * s + k] for s in range(slots)] for k in range(4)]

        def first_step(slot):
            arrived = before[slot][1] + before[slot][-1]
            return call(
                functools.partial(first_kernel, at(0), slots, slot, [b[1] for b in arrived], unit, per_block),
                [chunk] * 2,
                [SMEM, SMEM] + [VMEM] * (3 + len(arrived)),
                [VMEM] * 2,
                [table, places, start_block, high_t[slot], low_t[slot]] + [b[0] for b in arrived],
                flops=flops,
                name="first_product",
            )

        def column_step(chunks, older=None):
            out = []
            for slot in range(slots):
                others = chunks[:slot] + chunks[slot + 1 :]
                more = [] if older is None else [older[slot]]
                out.append(
                    call(
                        functools.partial(column_kernel, slots, slot, older is not None),
                        chunk,
                        [SMEM, SMEM] + [VMEM] * (3 + len(more)) + [ANY] * len(others),
                        VMEM,
                        [columns, scalars, high[slot], low[slot]] + more + [chunks[slot]] + others,
                        scratch=[
                            pltpu.VMEM(chunk.shape, jnp.float32),
                            pltpu.VMEM((len(others), size, vec), jnp.float32),
                            pltpu.SemaphoreType.DMA((len(others),)),
                        ],
                        flops=flops,
                        name="column_product",
                    )
                )
            return out

        def row_step(last, mine, pieces, got, vectors):
            return call(
                functools.partial(row_kernel, slots, pieces, last),
                [chunk] * slots,
                [SMEM] * 3 + [VMEM] * (4 * slots) + [ANY] * len(got),
                [VMEM] * slots,
                [table, places, scalars] + high_t + low_t + mine + vectors + got,
                scratch=[
                    pltpu.VMEM((slots, size, vec), jnp.float32),
                    pltpu.VMEM((len(got), size, vec), jnp.float32),
                    pltpu.SemaphoreType.DMA((len(got),)),
                ],
                flops=flops * slots,
                name="row_product",
            )

        xs, ps = zip(*[first_step(slot) for slot in range(slots)])
        xs, ps = list(xs), list(ps)
        qs = column_step(gather_row(ps))
        ps = list(row_step(False, qs, *gather_col(qs), xs))
        gs = column_step(gather_row(ps), qs)
        pieces, got = gather_col(gs)

        owner_pieces = [(at(0), slot, 0) for slot in range(slots)] + pieces
        following, gram_matrix = call(
            functools.partial(owner_kernel, slots, owner_pieces, unit, per_block),
            [jax.ShapeDtypeStruct(start_block.shape, jnp.float32), square],
            [SMEM] * 3 + [VMEM] + [ANY] * len(owner_pieces),
            [VMEM] * 2,
            [table, places, scalars, start_block] + gs + got,
            scratch=[
                pltpu.VMEM((len(owner_pieces), size, vec), jnp.float32),
                pltpu.SemaphoreType.DMA((len(owner_pieces),)),
            ],
            flops=6 * held_rows * vec * vec,
            name="owner_rows",
        )
        ps = list(row_step(True, gs, pieces, got, xs))
        across = [flip(p, "row", row_bits[-1]) for p in ps]
        gram_matrix = sum_over(gram_matrix, "row", row_bits[:-1])
        gram_matrix = sum_over(gram_matrix, "col", col_bits[0:1])
        gram_matrix, across = tie((gram_matrix, across))
        images = gather_rest(ps, across)
        gram_matrix = sum_over(gram_matrix, "col", col_bits[1:2])
        gram_matrix = sum_over(gram_matrix, "col", col_bits[2:])
        gram_matrix = sum_over(gram_matrix, "row", row_bits[-1:])
        inner_local = call(
            functools.partial(inner_kernel, slots),
            square,
            [SMEM, SMEM] + [VMEM] * len(images),
            VMEM,
            [columns, lax.axis_index("row").reshape(1)] + images,
            scratch=[
                pltpu.VMEM((len(images), size, vec), jnp.float32),
                pltpu.VMEM((len(images) * size, vec), jnp.float32),
            ],
            flops=6 * len(images) * size * vec * vec,
            name="inner_product",
        )
        inner_matrix = sum_over(inner_local, "col", col_bits)
        inverse = call(factor_kernel, square, [VMEM], VMEM, [gram_matrix], flops=4 * vec**3, name="factor")
        basis_block = call(
            basis_kernel,
            jax.ShapeDtypeStruct(start_block.shape, jnp.float32),
            [VMEM] * 2,
            VMEM,
            [following, inverse],
            flops=12 * held_rows * vec * vec,
            name="basis",
        )
        projected = call(project_kernel, square, [VMEM] * 2, VMEM, [inverse, inner_matrix], name="project")
        return (basis_block, projected)

    in_specs = (
        P(("row", "col"), None),
        P("row", "col", None, None),
        P("row", "col"),
        P("row", "col"),
        P("row", "col"),
        P(),
        P(),
    )
    out_specs = (P(("row", "col"), None), P())
    return jax.shard_map(body, mesh=mesh, in_specs=in_specs, out_specs=out_specs, check_vma=False)
```

```python
import functools

import jax
import jax.numpy as jnp
import numpy as np
from jax import lax
from jax.experimental import pallas as pl
from jax.experimental.pallas import tpu as pltpu
from jax.sharding import PartitionSpec as P

HIGHEST = lax.Precision.HIGHEST
PANEL = 8
VMEM = pl.BlockSpec(memory_space=pltpu.VMEM)
SMEM = pl.BlockSpec(memory_space=pltpu.SMEM)
ANY = pl.BlockSpec(memory_space=pl.ANY)


def call(kernel, out_shape, in_specs, out_specs, args, scratch=(), flops=0, name=None):
    moved = sum(a.size * a.dtype.itemsize for a in args)
    return pl.pallas_call(
        kernel,
        out_shape=out_shape,
        in_specs=in_specs,
        out_specs=out_specs,
        scratch_shapes=list(scratch),
        compiler_params=pltpu.CompilerParams(vmem_limit_bytes=40 * 1024 * 1024),
        cost_estimate=pl.CostEstimate(flops=flops, bytes_accessed=moved, transcendentals=0),
        name=name,
    )(*args)


def split(value):
    high = value.astype(jnp.bfloat16)
    return high, (value - high.astype(jnp.float32)).astype(jnp.bfloat16)


def dot3(left_high, left_low, right):
    right_high, right_low = split(right)
    dot = functools.partial(jnp.dot, preferred_element_type=jnp.float32)
    return dot(left_high, right_high) + (dot(left_high, right_low) + dot(left_low, right_high))


def self_product(value):
    high, low = split(value)

    def dot(left, right):
        return lax.dot_general(left, right, (((0,), (0,)), ((), ())), preferred_element_type=jnp.float32)

    mixed = dot(high, low)
    return dot(high, high) + (dot(low, low) + (mixed + mixed.T))


def prepare_kernel(slots, values, *outs):
    for s in range(slots):
        high, low, high_t, low_t = outs[4 * s : 4 * s + 4]
        high[...], low[...] = split(values[s])
        high_t[...], low_t[...] = split(values[s].T)


def table_row(table, places, entry, slots, slot):
    return table[places[entry] * slots + slot]


def pick(row, held, first_unit, unit, per_block, out, begin, base):
    vec = out.shape[1]
    count = held.shape[0] // unit
    for i in range(out.shape[0] // unit):
        value = jnp.zeros((unit, vec), out.dtype)
        for ref, ref_begin in base:
            at = begin + i * unit - ref_begin
            if 0 <= at < ref.shape[0]:
                value = value + ref[at : at + unit, :]
        local = row * per_block + begin // unit + i - first_unit
        valid = (row >= 0) & (local >= 0) & (local < count)
        rows = pl.ds(pl.multiple_of(jnp.clip(local, 0, count - 1) * unit, unit), unit)
        out[i * unit : (i + 1) * unit, :] = jnp.where(valid, held[rows, :], value)


def ring_kernel(entry, slots, slot, begin, befores, unit, per_block, table, places, held, *refs):
    base, out = list(zip(refs[:-1], befores)), refs[-1]
    pick(table_row(table, places, entry, slots, slot), held, places[0], unit, per_block, out, begin, base)


def first_kernel(entry, slots, slot, befores, unit, per_block, table, places, held, high_t, low_t, *refs):
    base, (x_out, p_out) = list(zip(refs[:-2], befores)), refs[-2:]
    pick(table_row(table, places, entry, slots, slot), held, places[0], unit, per_block, x_out, 0, base)
    p_out[...] = dot3(high_t[...], low_t[...], x_out[...])


def add_matching(hits, copies, total):
    for hit, (copy, _, _) in zip(hits, copies):

        @pl.when(hit)
        def _():
            copy.start()

    for hit, (copy, landing, rows) in zip(hits, copies):

        @pl.when(hit)
        def _():
            copy.wait()
            total[rows, :] += landing[...]


def column_kernel(slots, slot, last, columns, scalars, high, low, *refs):
    refs = list(refs)
    older = refs.pop(0) if last else None
    mine = refs.pop(0)
    arrived, (q_out, total, landing, sems) = refs[:-4], refs[-4:]
    center, radius = scalars[0], scalars[1]
    column = columns[slot]
    others = [k for k in range(len(arrived) + 1) if k != slot]
    hits, copies = [], []
    for i, k in enumerate(others):
        hits.append((columns[k] == column) & (column >= 0))
        copies.append(
            (pltpu.make_async_copy(arrived[i], landing.at[i], sems.at[i]), landing.at[i], slice(0, total.shape[0]))
        )
    total[...] = mine[...]
    add_matching(hits, copies, total)
    q = dot3(high[...], low[...], total[...])
    if last:
        q = (2.0 / radius) * (q - (center / radius) * older[...])
    q_out[...] = q


def row_kernel(slots, own, pieces, last, table, places, scalars, *refs):
    refs = list(refs)
    high_t, low_t, vectors = [refs.pop(0) for _ in range(3)]
    mine = [refs.pop(0) for _ in range(slots)]
    arrived, (p_out, total, landing, sems) = refs[: len(pieces)], refs[len(pieces) :]
    center, radius = scalars[0], scalars[1]
    wanted = table[own]
    rows = [table_row(table, places, entry, slots, slot) for entry, slot, _ in pieces]

    def copy(b):
        return pltpu.make_async_copy(arrived[b], landing.at[b, pl.ds(0, arrived[b].shape[0])], sems.at[b])

    def each(action):
        for b in range(len(pieces)):

            @pl.when((rows[b] == wanted) & (wanted >= 0))
            def _():
                action(b)

    each(lambda b: copy(b).start())
    total[...] = mine[own][...]
    for t in range(slots):
        if t != own:

            @pl.when((table[t] == wanted) & (wanted >= 0))
            def _():
                total[...] += mine[t][...]

    def add(b):
        copy(b).wait()
        first, count = pieces[b][2], arrived[b].shape[0]
        total[first : first + count, :] += landing[b, :count, :]

    each(add)
    if last:
        y = total[...] + (2.0 * (center / radius) * (center / radius) - 1.0) * vectors[...]
    else:
        y = (total[...] - center * vectors[...]) / radius
    p_out[...] = dot3(high_t[...], low_t[...], y)


def owner_kernel(slots, pieces, unit, per_block, table, places, scalars, start, *refs):
    arrived, (y_out, gram_out, landing, sems) = refs[:-4], refs[-4:]
    center, radius = scalars[0], scalars[1]
    held = y_out.shape[0] // unit

    def copy(b):
        return pltpu.make_async_copy(arrived[b], landing.at[b, pl.ds(0, arrived[b].shape[0])], sems.at[b])

    def each(action):
        for b, (entry, slot, first) in enumerate(pieces):
            row = table_row(table, places, entry, slots, slot)
            count = arrived[b].shape[0] // unit
            begin = row * per_block + first // unit - places[0]

            @pl.when((row >= 0) & (begin + count > 0) & (begin < held))
            def _():
                action(b, begin, count)

    each(lambda b, begin, count: copy(b).start())
    y_out[...] = (2.0 * (center / radius) * (center / radius) - 1.0) * start[...]

    def add(b, begin, count):
        copy(b).wait()
        for i in range(count):
            local = begin + i

            @pl.when((local >= 0) & (local < held))
            def _():
                rows = pl.ds(pl.multiple_of(jnp.clip(local, 0, held - 1) * unit, unit), unit)
                y_out[rows, :] += landing[b, i * unit : (i + 1) * unit, :]

    each(add)
    gram_out[...] = self_product(y_out[...])


def inner_kernel(slots, columns, place, *refs):
    arrived, out, order, total = refs[:-3], refs[-3], refs[-2], refs[-1]
    count, size = len(arrived), order.shape[1]
    for k, held in enumerate(arrived):
        order[lax.bitwise_xor(place[0], k // slots) * slots + k % slots] = held[...]
    ids = [columns[lax.bitwise_xor(place[0], i // slots) * slots + i % slots] for i in range(count)]
    for i in range(count):
        earlier = ids[i] < 0
        for k in range(i):
            earlier = earlier | (ids[k] == ids[i])
        total[i * size : (i + 1) * size, :] = jnp.where(earlier, 0.0, order[i])
        for k in range(i + 1, count):

            @pl.when((ids[k] == ids[i]) & jnp.logical_not(earlier))
            def _():
                total[i * size : (i + 1) * size, :] += order[k]

    out[...] = self_product(total[...])


def factor_kernel(gram, inverse_out):
    order = gram.shape[0]
    blocks = order // PANEL
    shape = (PANEL, order)
    below = lax.broadcasted_iota(jnp.int32, shape, 0)
    lane = lax.broadcasted_iota(jnp.int32, shape, 1)
    left = [gram[b * PANEL : (b + 1) * PANEL, :] for b in range(blocks)]
    right = [jnp.where(lane == below + b * PANEL, 1.0, 0.0) for b in range(blocks)]

    def spread(block, k):
        return jnp.broadcast_to(block[k : k + 1, :], shape)

    for b in range(blocks):
        rest = range(b, blocks)
        panel = [
            {i: jnp.broadcast_to(left[i][:, b * PANEL + j : b * PANEL + j + 1], shape) for i in rest}
            for j in range(PANEL)
        ]
        scale = jnp.ones(shape, jnp.float32)
        for k in range(PANEL):
            pivot = spread(panel[k][b], k)
            inverse = 1.0 / pivot
            scale = jnp.where(below == k, lax.rsqrt(pivot), scale)
            factor = {i: panel[k][i] * inverse for i in rest}
            factor[b] = jnp.where(below > k, factor[b], 0.0)
            left_row, right_row = spread(left[b], k), spread(right[b], k)
            for j in range(k + 1, PANEL):
                row = spread(panel[j][b], k)
                for i in rest:
                    panel[j][i] = panel[j][i] - factor[i] * row
            for i in rest:
                left[i] = left[i] - factor[i] * left_row
                right[i] = right[i] - factor[i] * right_row
        inverse_out[b * PANEL : (b + 1) * PANEL, :] = right[b] * scale


def basis_kernel(following, inverse, out):
    out[...] = dot3(*split(following[...]), inverse[...].T)


def project_kernel(inverse, inner, out):
    half = dot3(*split(inverse[...]), inner[...])
    out[...] = dot3(*split(half), inverse[...].T)


def solution(mesh):
    n_row, n_col = mesh.shape["row"], mesh.shape["col"]
    tie = lax.optimization_barrier
    far = n_col // 2

    ring = list(range(0, n_col, 2)) + list(range(1, n_col, 2))[::-1]
    position = {col: k for k, col in enumerate(ring)}

    place_lines = np.array(
        [[0] + [col ^ ring[(position[col] + d) % n_col] for d in range(-far, far + 1)] for col in range(n_col)], np.int32
    )

    def at(distance):
        return far + 1 + distance

    def forward(value, step):
        return lax.ppermute(value, "col", [(col, ring[(k + step) % n_col]) for k, col in enumerate(ring)])

    def shares(distance, size):
        if 2 * distance < n_col:
            return (1, 0, size), (-1, 0, size)
        return (1, 0, size // 2), (-1, size // 2, size)

    def flip(value, axis, bit):
        size = n_row if axis == "row" else n_col
        return lax.ppermute(value, axis, [(i, i ^ bit) for i in range(size)])

    def table_over(own, axis):
        for bit in powers(n_row if axis == "row" else n_col):
            own = jnp.concatenate([own, flip(own, axis, bit)])
        return own

    def gather_rest(own, across):
        top = powers(n_row)[-1]
        held = {0: own, top: across}
        bit = top // 2
        while bit:
            held.update({j ^ bit: [flip(v, "row", bit) for v in values] for j, values in list(held.items())})
            bit //= 2
        return sum([held[j] for j in range(n_row)], [])

    def gather_row(own):
        return gather_rest(own, [flip(value, "row", powers(n_row)[-1]) for value in own])

    def sum_over(value, axis, bits):
        for bit in bits:
            value = value + flip(value, axis, bit)
        return value

    def powers(size):
        return [1 << k for k in range(size.bit_length() - 1)]

    def gather_col(own):
        held = [{1: value, -1: value} for value in own]
        pieces, got = [], []
        for distance in range(1, far + 1):
            for slot, value in enumerate(own):
                for step, first, end in shares(distance, value.shape[0]):
                    chunk = held[slot][step]
                    if end - first < chunk.shape[0]:
                        chunk = chunk[first:end]
                    held[slot][step] = forward(chunk, step)
                    pieces.append((at(-step * distance), slot, first))
                    got.append(held[slot][step])
        return pieces, got

    def body(start_block, block_values, block_rows, block_cols, block_count, center, radius):
        values = block_values[0]
        slots, size, _ = values.shape
        held_rows, vec = start_block.shape
        unit = min(size // 2, held_rows)
        per_block = size // unit
        live = jnp.arange(slots) < block_count[0, 0]
        rows = jnp.where(live, block_rows[0], -1)
        cols = jnp.where(live, block_cols[0], -1)
        col = lax.axis_index("col")
        with jax.named_scope("tables"):
            table = table_over(rows, "col")
            columns = table_over(cols, "row")
        places = jnp.asarray(place_lines)[col]
        places = places.at[0].set(col * (held_rows // unit))
        scalars = jnp.concatenate([center, radius])
        row_bits, col_bits = powers(n_row), powers(n_col)

        chunk = jax.ShapeDtypeStruct((size, vec), jnp.float32)
        square = jax.ShapeDtypeStruct((vec, vec), jnp.float32)
        half_block = jax.ShapeDtypeStruct((size, size), jnp.bfloat16)
        blocks = call(
            functools.partial(prepare_kernel, slots),
            [half_block] * (4 * slots),
            [VMEM],
            [VMEM] * (4 * slots),
            [values],
            name="split_blocks",
        )
        flops = 6 * size * size * vec

        before = [{1: [], -1: []} for _ in range(slots)]
        for distance in range(far, 0, -1):
            for slot in range(slots):
                for step, first, end in shares(distance, size):
                    prior = before[slot][step]
                    value = call(
                        functools.partial(
                            ring_kernel, at(step * distance), slots, slot, first, [b[1] for b in prior], unit, per_block
                        ),
                        jax.ShapeDtypeStruct((end - first, vec), jnp.float32),
                        [SMEM, SMEM] + [VMEM] * (1 + len(prior)),
                        VMEM,
                        [table, places, start_block] + [b[0] for b in prior],
                        name="pick_rows",
                    )
                    before[slot][step] = [(forward(value, step), first)]
            if distance == 2:
                value, first = before[0][1][0]
                value, columns, blocks = tie((value, columns, blocks))
                before[0][1] = [(value, first)]
        high, low, high_t, low_t = [[blocks[4 * s + k] for s in range(slots)] for k in range(4)]

        def first_step(slot):
            arrived = before[slot][1] + before[slot][-1]
            return call(
                functools.partial(first_kernel, at(0), slots, slot, [b[1] for b in arrived], unit, per_block),
                [chunk] * 2,
                [SMEM, SMEM] + [VMEM] * (3 + len(arrived)),
                [VMEM] * 2,
                [table, places, start_block, high_t[slot], low_t[slot]] + [b[0] for b in arrived],
                flops=flops,
                name="first_product",
            )

        def column_step(chunks, older=None):
            out = []
            for slot in range(slots):
                others = chunks[:slot] + chunks[slot + 1 :]
                more = [] if older is None else [older[slot]]
                out.append(
                    call(
                        functools.partial(column_kernel, slots, slot, older is not None),
                        chunk,
                        [SMEM, SMEM] + [VMEM] * (3 + len(more)) + [ANY] * len(others),
                        VMEM,
                        [columns, scalars, high[slot], low[slot]] + more + [chunks[slot]] + others,
                        scratch=[
                            pltpu.VMEM(chunk.shape, jnp.float32),
                            pltpu.VMEM((len(others), size, vec), jnp.float32),
                            pltpu.SemaphoreType.DMA((len(others),)),
                        ],
                        flops=flops,
                        name="column_product",
                    )
                )
            return out

        def row_step(last, mine, pieces, got, vectors):
            return [
                call(
                    functools.partial(row_kernel, slots, slot, pieces, last),
                    chunk,
                    [SMEM] * 3 + [VMEM] * (3 + slots) + [ANY] * len(got),
                    VMEM,
                    [table, places, scalars, high_t[slot], low_t[slot], vectors[slot]] + mine + got,
                    scratch=[
                        pltpu.VMEM(chunk.shape, jnp.float32),
                        pltpu.VMEM((len(got), size, vec), jnp.float32),
                        pltpu.SemaphoreType.DMA((len(got),)),
                    ],
                    flops=flops,
                    name="row_product",
                )
                for slot in range(slots)
            ]

        xs, ps = zip(*[first_step(slot) for slot in range(slots)])
        xs, ps = list(xs), list(ps)
        qs = column_step(gather_row(ps))
        ps = list(row_step(False, qs, *gather_col(qs), xs))
        gs = column_step(gather_row(ps), qs)
        pieces, got = gather_col(gs)

        owner_pieces = [(at(0), slot, 0) for slot in range(slots)] + pieces
        following, gram_matrix = call(
            functools.partial(owner_kernel, slots, owner_pieces, unit, per_block),
            [jax.ShapeDtypeStruct(start_block.shape, jnp.float32), square],
            [SMEM] * 3 + [VMEM] + [ANY] * len(owner_pieces),
            [VMEM] * 2,
            [table, places, scalars, start_block] + gs + got,
            scratch=[
                pltpu.VMEM((len(owner_pieces), size, vec), jnp.float32),
                pltpu.SemaphoreType.DMA((len(owner_pieces),)),
            ],
            flops=6 * held_rows * vec * vec,
            name="owner_rows",
        )
        ps = list(row_step(True, gs, pieces, got, xs))
        across = [flip(p, "row", row_bits[-1]) for p in ps]
        gram_matrix = sum_over(gram_matrix, "row", row_bits[:-1])
        gram_matrix = sum_over(gram_matrix, "col", col_bits[0:1])
        gram_matrix, across = tie((gram_matrix, across))
        images = gather_rest(ps, across)
        gram_matrix = sum_over(gram_matrix, "col", col_bits[1:2])
        gram_matrix = sum_over(gram_matrix, "col", col_bits[2:])
        gram_matrix = sum_over(gram_matrix, "row", row_bits[-1:])
        inner_local = call(
            functools.partial(inner_kernel, slots),
            square,
            [SMEM, SMEM] + [VMEM] * len(images),
            VMEM,
            [columns, lax.axis_index("row").reshape(1)] + images,
            scratch=[
                pltpu.VMEM((len(images), size, vec), jnp.float32),
                pltpu.VMEM((len(images) * size, vec), jnp.float32),
            ],
            flops=6 * len(images) * size * vec * vec,
            name="inner_product",
        )
        inner_matrix = sum_over(inner_local, "col", col_bits)
        inverse = call(factor_kernel, square, [VMEM], VMEM, [gram_matrix], flops=4 * vec**3, name="factor")
        basis_block = call(
            basis_kernel,
            jax.ShapeDtypeStruct(start_block.shape, jnp.float32),
            [VMEM] * 2,
            VMEM,
            [following, inverse],
            flops=12 * held_rows * vec * vec,
            name="basis",
        )
        projected = call(project_kernel, square, [VMEM] * 2, VMEM, [inverse, inner_matrix], name="project")
        return (basis_block, projected)

    in_specs = (
        P(("row", "col"), None),
        P("row", "col", None, None),
        P("row", "col"),
        P("row", "col"),
        P("row", "col"),
        P(),
        P(),
    )
    out_specs = (P(("row", "col"), None), P())
    return jax.shard_map(body, mesh=mesh, in_specs=in_specs, out_specs=out_specs, check_vma=False)
```

```python
import functools

import jax
import jax.numpy as jnp
import numpy as np
from jax import lax
from jax.experimental import pallas as pl
from jax.experimental.pallas import tpu as pltpu
from jax.sharding import PartitionSpec as P

HIGHEST = lax.Precision.HIGHEST
PANEL = 8
VMEM = pl.BlockSpec(memory_space=pltpu.VMEM)
SMEM = pl.BlockSpec(memory_space=pltpu.SMEM)
ANY = pl.BlockSpec(memory_space=pl.ANY)


def call(kernel, out_shape, in_specs, out_specs, args, scratch=(), flops=0, name=None):
    moved = sum(a.size * a.dtype.itemsize for a in args)
    return pl.pallas_call(
        kernel,
        out_shape=out_shape,
        in_specs=in_specs,
        out_specs=out_specs,
        scratch_shapes=list(scratch),
        compiler_params=pltpu.CompilerParams(vmem_limit_bytes=40 * 1024 * 1024),
        cost_estimate=pl.CostEstimate(flops=flops, bytes_accessed=moved, transcendentals=0),
        name=name,
    )(*args)


def split(value):
    high = value.astype(jnp.bfloat16)
    return high, (value - high.astype(jnp.float32)).astype(jnp.bfloat16)


def dot3(left_high, left_low, right):
    right_high, right_low = split(right)
    dot = functools.partial(jnp.dot, preferred_element_type=jnp.float32)
    return dot(left_high, right_high) + (dot(left_high, right_low) + dot(left_low, right_high))


def self_product(value):
    high, low = split(value)

    def dot(left, right):
        return lax.dot_general(left, right, (((0,), (0,)), ((), ())), preferred_element_type=jnp.float32)

    mixed = dot(high, low)
    return dot(high, high) + (mixed + mixed.T)


def prepare_kernel(slots, values, *outs):
    for s in range(slots):
        high, low, high_t, low_t = outs[4 * s : 4 * s + 4]
        high[...], low[...] = split(values[s])
        high_t[...], low_t[...] = split(values[s].T)


def table_row(table, places, entry, slots, slot):
    return table[places[entry] * slots + slot]


def pick(row, held, first_unit, unit, per_block, out, begin, base):
    vec = out.shape[1]
    count = held.shape[0] // unit
    for i in range(out.shape[0] // unit):
        value = jnp.zeros((unit, vec), out.dtype)
        for ref, ref_begin in base:
            at = begin + i * unit - ref_begin
            if 0 <= at < ref.shape[0]:
                value = value + ref[at : at + unit, :]
        local = row * per_block + begin // unit + i - first_unit
        valid = (row >= 0) & (local >= 0) & (local < count)
        rows = pl.ds(pl.multiple_of(jnp.clip(local, 0, count - 1) * unit, unit), unit)
        out[i * unit : (i + 1) * unit, :] = jnp.where(valid, held[rows, :], value)


def ring_kernel(entry, slots, slot, begin, befores, unit, per_block, table, places, held, *refs):
    base, out = list(zip(refs[:-1], befores)), refs[-1]
    pick(table_row(table, places, entry, slots, slot), held, places[0], unit, per_block, out, begin, base)


def first_kernel(entry, slots, slot, befores, unit, per_block, table, places, held, high_t, low_t, *refs):
    base, (x_out, p_out) = list(zip(refs[:-2], befores)), refs[-2:]
    pick(table_row(table, places, entry, slots, slot), held, places[0], unit, per_block, x_out, 0, base)
    p_out[...] = dot3(high_t[...], low_t[...], x_out[...])


def add_matching(hits, copies, total):
    for hit, (copy, _, _) in zip(hits, copies):

        @pl.when(hit)
        def _():
            copy.start()

    for hit, (copy, landing, rows) in zip(hits, copies):

        @pl.when(hit)
        def _():
            copy.wait()
            total[rows, :] += landing[...]


def column_kernel(slots, slot, last, columns, scalars, high, low, *refs):
    refs = list(refs)
    older = refs.pop(0) if last else None
    mine = refs.pop(0)
    arrived, (q_out, total, landing, sems) = refs[:-4], refs[-4:]
    center, radius = scalars[0], scalars[1]
    column = columns[slot]
    others = [k for k in range(len(arrived) + 1) if k != slot]
    hits, copies = [], []
    for i, k in enumerate(others):
        hits.append((columns[k] == column) & (column >= 0))
        copies.append(
            (pltpu.make_async_copy(arrived[i], landing.at[i], sems.at[i]), landing.at[i], slice(0, total.shape[0]))
        )
    total[...] = mine[...]
    add_matching(hits, copies, total)
    q = dot3(high[...], low[...], total[...])
    if last:
        q = (2.0 / radius) * (q - (center / radius) * older[...])
    q_out[...] = q


def row_kernel(slots, own, pieces, last, table, places, scalars, *refs):
    refs = list(refs)
    high_t, low_t, vectors = [refs.pop(0) for _ in range(3)]
    mine = [refs.pop(0) for _ in range(slots)]
    arrived, (p_out, total, landing, sems) = refs[: len(pieces)], refs[len(pieces) :]
    center, radius = scalars[0], scalars[1]
    wanted = table[own]
    rows = [table_row(table, places, entry, slots, slot) for entry, slot, _ in pieces]

    def copy(b):
        return pltpu.make_async_copy(arrived[b], landing.at[b, pl.ds(0, arrived[b].shape[0])], sems.at[b])

    def each(action):
        for b in range(len(pieces)):

            @pl.when((rows[b] == wanted) & (wanted >= 0))
            def _():
                action(b)

    each(lambda b: copy(b).start())
    total[...] = mine[own][...]
    for t in range(slots):
        if t != own:

            @pl.when((table[t] == wanted) & (wanted >= 0))
            def _():
                total[...] += mine[t][...]

    def add(b):
        copy(b).wait()
        first, count = pieces[b][2], arrived[b].shape[0]
        total[first : first + count, :] += landing[b, :count, :]

    each(add)
    if last:
        y = total[...] + (2.0 * (center / radius) * (center / radius) - 1.0) * vectors[...]
    else:
        y = (total[...] - center * vectors[...]) / radius
    p_out[...] = dot3(high_t[...], low_t[...], y)


def owner_kernel(slots, pieces, unit, per_block, table, places, scalars, start, *refs):
    arrived, (y_out, gram_out, landing, sems) = refs[:-4], refs[-4:]
    center, radius = scalars[0], scalars[1]
    held = y_out.shape[0] // unit

    def copy(b):
        return pltpu.make_async_copy(arrived[b], landing.at[b, pl.ds(0, arrived[b].shape[0])], sems.at[b])

    def each(action):
        for b, (entry, slot, first) in enumerate(pieces):
            row = table_row(table, places, entry, slots, slot)
            count = arrived[b].shape[0] // unit
            begin = row * per_block + first // unit - places[0]

            @pl.when((row >= 0) & (begin + count > 0) & (begin < held))
            def _():
                action(b, begin, count)

    each(lambda b, begin, count: copy(b).start())
    y_out[...] = (2.0 * (center / radius) * (center / radius) - 1.0) * start[...]

    def add(b, begin, count):
        copy(b).wait()
        for i in range(count):
            local = begin + i

            @pl.when((local >= 0) & (local < held))
            def _():
                rows = pl.ds(pl.multiple_of(jnp.clip(local, 0, held - 1) * unit, unit), unit)
                y_out[rows, :] += landing[b, i * unit : (i + 1) * unit, :]

    each(add)
    gram_out[...] = self_product(y_out[...])


def inner_kernel(slots, columns, place, *refs):
    arrived, out, order, total = refs[:-3], refs[-3], refs[-2], refs[-1]
    count, size = len(arrived), order.shape[1]
    for k, held in enumerate(arrived):
        order[lax.bitwise_xor(place[0], k // slots) * slots + k % slots] = held[...]
    ids = [columns[lax.bitwise_xor(place[0], i // slots) * slots + i % slots] for i in range(count)]
    for i in range(count):
        earlier = ids[i] < 0
        for k in range(i):
            earlier = earlier | (ids[k] == ids[i])
        total[i * size : (i + 1) * size, :] = jnp.where(earlier, 0.0, order[i])
        for k in range(i + 1, count):

            @pl.when((ids[k] == ids[i]) & jnp.logical_not(earlier))
            def _():
                total[i * size : (i + 1) * size, :] += order[k]

    out[...] = self_product(total[...])


def factor_kernel(gram, inverse_out):
    order = gram.shape[0]
    blocks = order // PANEL
    shape = (PANEL, order)
    below = lax.broadcasted_iota(jnp.int32, shape, 0)
    lane = lax.broadcasted_iota(jnp.int32, shape, 1)
    left = [gram[b * PANEL : (b + 1) * PANEL, :] for b in range(blocks)]
    right = [jnp.where(lane == below + b * PANEL, 1.0, 0.0) for b in range(blocks)]

    def spread(block, k):
        return jnp.broadcast_to(block[k : k + 1, :], shape)

    for b in range(blocks):
        rest = range(b, blocks)
        panel = [
            {i: jnp.broadcast_to(left[i][:, b * PANEL + j : b * PANEL + j + 1], shape) for i in rest}
            for j in range(PANEL)
        ]
        scale = jnp.ones(shape, jnp.float32)
        for k in range(PANEL):
            pivot = spread(panel[k][b], k)
            inverse = 1.0 / pivot
            scale = jnp.where(below == k, lax.rsqrt(pivot), scale)
            factor = {i: panel[k][i] * inverse for i in rest}
            factor[b] = jnp.where(below > k, factor[b], 0.0)
            left_row, right_row = spread(left[b], k), spread(right[b], k)
            for j in range(k + 1, PANEL):
                row = spread(panel[j][b], k)
                for i in rest:
                    panel[j][i] = panel[j][i] - factor[i] * row
            for i in rest:
                left[i] = left[i] - factor[i] * left_row
                right[i] = right[i] - factor[i] * right_row
        inverse_out[b * PANEL : (b + 1) * PANEL, :] = right[b] * scale


def basis_kernel(following, inverse, out):
    out[...] = dot3(*split(following[...]), inverse[...].T)


def project_kernel(inverse, inner, out):
    half = dot3(*split(inverse[...]), inner[...])
    out[...] = dot3(*split(half), inverse[...].T)


def solution(mesh):
    n_row, n_col = mesh.shape["row"], mesh.shape["col"]
    tie = lax.optimization_barrier
    far = n_col // 2

    ring = list(range(0, n_col, 2)) + list(range(1, n_col, 2))[::-1]
    position = {col: k for k, col in enumerate(ring)}

    place_lines = np.array(
        [[0] + [col ^ ring[(position[col] + d) % n_col] for d in range(-far, far + 1)] for col in range(n_col)], np.int32
    )

    def at(distance):
        return far + 1 + distance

    def forward(value, step):
        return lax.ppermute(value, "col", [(col, ring[(k + step) % n_col]) for k, col in enumerate(ring)])

    def shares(distance, size):
        if 2 * distance < n_col:
            return (1, 0, size), (-1, 0, size)
        return (1, 0, size // 2), (-1, size // 2, size)

    def flip(value, axis, bit):
        size = n_row if axis == "row" else n_col
        return lax.ppermute(value, axis, [(i, i ^ bit) for i in range(size)])

    def table_over(own, axis):
        for bit in powers(n_row if axis == "row" else n_col):
            own = jnp.concatenate([own, flip(own, axis, bit)])
        return own

    def gather_rest(own, across):
        top = powers(n_row)[-1]
        held = {0: own, top: across}
        bit = top // 2
        while bit:
            held.update({j ^ bit: [flip(v, "row", bit) for v in values] for j, values in list(held.items())})
            bit //= 2
        return sum([held[j] for j in range(n_row)], [])

    def gather_row(own):
        return gather_rest(own, [flip(value, "row", powers(n_row)[-1]) for value in own])

    def sum_over(value, axis, bits):
        for bit in bits:
            value = value + flip(value, axis, bit)
        return value

    def powers(size):
        return [1 << k for k in range(size.bit_length() - 1)]

    def gather_col(own):
        held = [{1: value, -1: value} for value in own]
        pieces, got = [], []
        for distance in range(1, far + 1):
            for slot, value in enumerate(own):
                for step, first, end in shares(distance, value.shape[0]):
                    chunk = held[slot][step]
                    if end - first < chunk.shape[0]:
                        chunk = chunk[first:end]
                    held[slot][step] = forward(chunk, step)
                    pieces.append((at(-step * distance), slot, first))
                    got.append(held[slot][step])
        return pieces, got

    def body(start_block, block_values, block_rows, block_cols, block_count, center, radius):
        values = block_values[0]
        slots, size, _ = values.shape
        held_rows, vec = start_block.shape
        unit = min(size // 2, held_rows)
        per_block = size // unit
        live = jnp.arange(slots) < block_count[0, 0]
        rows = jnp.where(live, block_rows[0], -1)
        cols = jnp.where(live, block_cols[0], -1)
        col = lax.axis_index("col")
        with jax.named_scope("tables"):
            table = table_over(rows, "col")
            columns = table_over(cols, "row")
        places = jnp.asarray(place_lines)[col]
        places = places.at[0].set(col * (held_rows // unit))
        scalars = jnp.concatenate([center, radius])
        row_bits, col_bits = powers(n_row), powers(n_col)

        chunk = jax.ShapeDtypeStruct((size, vec), jnp.float32)
        square = jax.ShapeDtypeStruct((vec, vec), jnp.float32)
        half_block = jax.ShapeDtypeStruct((size, size), jnp.bfloat16)
        blocks = call(
            functools.partial(prepare_kernel, slots),
            [half_block] * (4 * slots),
            [VMEM],
            [VMEM] * (4 * slots),
            [values],
            name="split_blocks",
        )
        flops = 6 * size * size * vec

        before = [{1: [], -1: []} for _ in range(slots)]
        for distance in range(far, 0, -1):
            for slot in range(slots):
                for step, first, end in shares(distance, size):
                    prior = before[slot][step]
                    value = call(
                        functools.partial(
                            ring_kernel, at(step * distance), slots, slot, first, [b[1] for b in prior], unit, per_block
                        ),
                        jax.ShapeDtypeStruct((end - first, vec), jnp.float32),
                        [SMEM, SMEM] + [VMEM] * (1 + len(prior)),
                        VMEM,
                        [table, places, start_block] + [b[0] for b in prior],
                        name="pick_rows",
                    )
                    before[slot][step] = [(forward(value, step), first)]
            if distance == 2:
                value, first = before[0][1][0]
                value, columns, blocks = tie((value, columns, blocks))
                before[0][1] = [(value, first)]
        high, low, high_t, low_t = [[blocks[4 * s + k] for s in range(slots)] for k in range(4)]

        def first_step(slot):
            arrived = before[slot][1] + before[slot][-1]
            return call(
                functools.partial(first_kernel, at(0), slots, slot, [b[1] for b in arrived], unit, per_block),
                [chunk] * 2,
                [SMEM, SMEM] + [VMEM] * (3 + len(arrived)),
                [VMEM] * 2,
                [table, places, start_block, high_t[slot], low_t[slot]] + [b[0] for b in arrived],
                flops=flops,
                name="first_product",
            )

        def column_step(chunks, older=None):
            out = []
            for slot in range(slots):
                others = chunks[:slot] + chunks[slot + 1 :]
                more = [] if older is None else [older[slot]]
                out.append(
                    call(
                        functools.partial(column_kernel, slots, slot, older is not None),
                        chunk,
                        [SMEM, SMEM] + [VMEM] * (3 + len(more)) + [ANY] * len(others),
                        VMEM,
                        [columns, scalars, high[slot], low[slot]] + more + [chunks[slot]] + others,
                        scratch=[
                            pltpu.VMEM(chunk.shape, jnp.float32),
                            pltpu.VMEM((len(others), size, vec), jnp.float32),
                            pltpu.SemaphoreType.DMA((len(others),)),
                        ],
                        flops=flops,
                        name="column_product",
                    )
                )
            return out

        def row_step(last, mine, pieces, got, vectors):
            return [
                call(
                    functools.partial(row_kernel, slots, slot, pieces, last),
                    chunk,
                    [SMEM] * 3 + [VMEM] * (3 + slots) + [ANY] * len(got),
                    VMEM,
                    [table, places, scalars, high_t[slot], low_t[slot], vectors[slot]] + mine + got,
                    scratch=[
                        pltpu.VMEM(chunk.shape, jnp.float32),
                        pltpu.VMEM((len(got), size, vec), jnp.float32),
                        pltpu.SemaphoreType.DMA((len(got),)),
                    ],
                    flops=flops,
                    name="row_product",
                )
                for slot in range(slots)
            ]

        xs, ps = zip(*[first_step(slot) for slot in range(slots)])
        xs, ps = list(xs), list(ps)
        qs = column_step(gather_row(ps))
        ps = list(row_step(False, qs, *gather_col(qs), xs))
        gs = column_step(gather_row(ps), qs)
        pieces, got = gather_col(gs)

        owner_pieces = [(at(0), slot, 0) for slot in range(slots)] + pieces
        following, gram_matrix = call(
            functools.partial(owner_kernel, slots, owner_pieces, unit, per_block),
            [jax.ShapeDtypeStruct(start_block.shape, jnp.float32), square],
            [SMEM] * 3 + [VMEM] + [ANY] * len(owner_pieces),
            [VMEM] * 2,
            [table, places, scalars, start_block] + gs + got,
            scratch=[
                pltpu.VMEM((len(owner_pieces), size, vec), jnp.float32),
                pltpu.SemaphoreType.DMA((len(owner_pieces),)),
            ],
            flops=6 * held_rows * vec * vec,
            name="owner_rows",
        )
        ps = list(row_step(True, gs, pieces, got, xs))
        across = [flip(p, "row", row_bits[-1]) for p in ps]
        gram_matrix = sum_over(gram_matrix, "row", row_bits[:-1])
        gram_matrix = sum_over(gram_matrix, "col", col_bits[0:1])
        gram_matrix, across = tie((gram_matrix, across))
        images = gather_rest(ps, across)
        gram_matrix = sum_over(gram_matrix, "col", col_bits[1:2])
        gram_matrix = sum_over(gram_matrix, "col", col_bits[2:])
        gram_matrix = sum_over(gram_matrix, "row", row_bits[-1:])
        inner_local = call(
            functools.partial(inner_kernel, slots),
            square,
            [SMEM, SMEM] + [VMEM] * len(images),
            VMEM,
            [columns, lax.axis_index("row").reshape(1)] + images,
            scratch=[
                pltpu.VMEM((len(images), size, vec), jnp.float32),
                pltpu.VMEM((len(images) * size, vec), jnp.float32),
            ],
            flops=6 * len(images) * size * vec * vec,
            name="inner_product",
        )
        inner_matrix = sum_over(inner_local, "col", col_bits)
        inverse = call(factor_kernel, square, [VMEM], VMEM, [gram_matrix], flops=4 * vec**3, name="factor")
        basis_block = call(
            basis_kernel,
            jax.ShapeDtypeStruct(start_block.shape, jnp.float32),
            [VMEM] * 2,
            VMEM,
            [following, inverse],
            flops=12 * held_rows * vec * vec,
            name="basis",
        )
        projected = call(project_kernel, square, [VMEM] * 2, VMEM, [inverse, inner_matrix], name="project")
        return (basis_block, projected)

    in_specs = (
        P(("row", "col"), None),
        P("row", "col", None, None),
        P("row", "col"),
        P("row", "col"),
        P("row", "col"),
        P(),
        P(),
    )
    out_specs = (P(("row", "col"), None), P())
    return jax.shard_map(body, mesh=mesh, in_specs=in_specs, out_specs=out_specs, check_vma=False)
```
